512 devices in a mesh: prompt: 8 (over z_lo, core), resp: 16 (over z_hi, x), tensor: 4 (over y).
Axes of the slice: x: 4, y: 4, z: 16 (z_hi: 4, z_lo: 4; z = z_hi * 4 + z_lo), core: 2. Of those that a mesh axis runs over, the one named last changes fastest.
Arguments:
- queries: bfloat16 [128, 2, 64, 96, 128], P(('prompt', 'resp'), None, None, 'tensor'), may hold values from -192 to 192
- resp_kv: bfloat16 [128, 2, 64, 8, 2, 128], P(('prompt', 'resp'), None, None, 'tensor'), may hold values from -6 to 6
- prompt_kv: bfloat16 [16, 1024, 8, 2, 128], P('resp', 'prompt', 'tensor'), may hold values from -6 to 6
- prompt_of: int32 [128], replicated, may hold values from 0 to 15
- prompt_len: int32 [16], replicated, may hold values from 1 to 8, as said below
- reward_head: float32 [96, 128], P('tensor'), may hold values from -0.0546875 to 0.0546875
Outputs:
- pair_loss: float32 [128], P(('prompt', 'resp'))
- grad_query: bfloat16 [128, 2, 64, 96, 128], P(('prompt', 'resp'), None, None, 'tensor')
- grad_resp_kv: bfloat16 [128, 2, 64, 8, 2, 128], P(('prompt', 'resp'), None, None, 'tensor')
- grad_prompt_kv: bfloat16 [16, 1024, 8, 2, 128], P('resp', 'prompt', 'tensor')
The draws below stay inside these ranges and needn't reach their ends.
Inputs may be any that keep to these rules, and one draw needn't show every extreme that they name: `prompt_len`: at least one prompt has all 8 blocks.
All inputs are finite; a program needn't handle non-finite values.
Results may differ from the reference program's by a relative error of at most 0.025.
Values may be sent and summed in bfloat16 or wider, within the bound.
A program may use at most 128 MiB of HBM per device.

```python
import math
import jax
import jax.numpy as jnp
import numpy as np
from jax import lax

H = 96
KVH = 8
HD = 128
BLOCK = 128
RTOK = 64
PTOK = 1024
PBLK = 8
NPROM = 16
NPAIR = 128


strengths = (12.0, 20.0, 32.0)


def shared_resp(key):
    shape = (NPAIR, 2, RTOK, KVH, 2, HD)
    base = jax.random.truncated_normal(key, -6.0, 6.0, shape, jnp.float32)
    for index, strength in enumerate(strengths):
        factor = 1.0 - 2.0 / (strength * math.sqrt(HD))
        base = base.at[:, :, 2 * index + 1, :, 0, :].set(base[:, :, 2 * index, :, 0, :] * factor)
    return base


def draw_resp_kv(key, part):
    shared = shared_resp(key)
    return shared.astype(jnp.bfloat16)


def draw_queries(key, part):
    shared = shared_resp(key)
    key = jax.random.fold_in(key, 11)
    base = jax.random.truncated_normal(key, -6.0, 6.0, (NPAIR, 2, RTOK, H, HD), jnp.float32)
    group_size = H // KVH
    for index, strength in enumerate(strengths):
        aligned = strength * shared[:, :, 2 * index, :, 0, :]
        aligned = jnp.repeat(aligned, group_size, axis=2)
        base = base.at[:, :, RTOK - 1 - index].set(aligned)
    return base.astype(jnp.bfloat16)


def draw_prompt_len(key, part):
    key = jax.random.fold_in(key, 5)
    key_lengths, key_longest = jax.random.split(key)
    lengths = jax.random.randint(key_lengths, (NPROM,), 1, PBLK + 1)
    longest = jax.random.randint(key_longest, (), 0, NPROM)
    return jnp.where(jnp.arange(NPROM) == longest, PBLK, lengths).astype(jnp.int32)


def touch_ends(array, key, smallest, top_value):
    spot = [jax.random.randint(jax.random.fold_in(key, axis), (), 0, length) for axis, length in enumerate(array.shape)]
    widest = array.shape.index(max(array.shape))
    next_to = spot[:widest] + [(spot[widest] + 1) % array.shape[widest]] + spot[widest + 1:]
    return array.at[tuple(spot)].set(smallest).at[tuple(next_to)].set(top_value)


def level_of(key, dims, cuts, least, top_value):
    gain = 1.0
    for position, blocks in cuts:
        heights = jax.random.uniform(jax.random.fold_in(jax.random.fold_in(key, 6), position), (blocks,), jnp.float32, least / len(cuts), top_value / len(cuts))
        gain = gain * jnp.repeat(jnp.exp(heights), dims[position] // blocks).reshape((-1,) + (1,) * (len(dims) - 1 - position))
    return gain


def cumulative_ranks(count, lean):
    loads = [(1 << 20) // math.isqrt(grade ** lean) + 1 for grade in range(1, count + 1)]
    scale = 1 + sum(loads) // (1 << 30)
    return np.cumsum(np.array([max(1, weight // scale) for weight in loads]))


def skewed_ids(key, shape, count, lean):
    listing = cumulative_ranks(count, lean)
    lot = jax.random.randint(jax.random.fold_in(key, 1), shape, 0, int(listing[count - 1]))
    rank = jnp.searchsorted(jnp.asarray(listing, jnp.int32), lot, side="right")
    return jax.random.permutation(jax.random.fold_in(key, 2), count)[rank].astype(jnp.int32)


def centred(stream_key, extent, scale, reach, cuts=(), dtype=jnp.bfloat16):
    gain = level_of(stream_key, extent, cuts, -0.22, 0.18) if cuts else 1.0
    entries = jax.random.normal(stream_key, extent, jnp.float32) * scale * gain
    return jnp.minimum(jnp.maximum(entries, -reach), reach).astype(dtype)


def setup_inputs(seed: int = 0) -> dict:
    seeds = jax.random.split(jax.random.key(seed), 7)
    queries = draw_queries(jax.random.fold_in(seeds[6], 71), 0)
    resp_kv = draw_resp_kv(jax.random.fold_in(seeds[6], 71), 0)
    prompt_kv = centred(seeds[2], (NPROM, PTOK, KVH, 2, HD), 1.0, 6.0, ((0, 16), (1, 8), (2, 4)))
    prompt_of = touch_ends(skewed_ids(seeds[3], (NPAIR,), NPROM, 2), jax.random.fold_in(seeds[3], 3), 0, NPROM - 1).astype(jnp.int32)
    prompt_len = draw_prompt_len(jax.random.fold_in(seeds[6], 71), 0)
    reward_head = centred(seeds[5], (H, HD), (H * HD) ** -0.5, 0.0546875, ((0, 4),), jnp.float32)
    return {"queries": queries, "resp_kv": resp_kv, "prompt_kv": prompt_kv, "prompt_of": prompt_of, "prompt_len": prompt_len, "reward_head": reward_head}


loss_scale = 8192.0


def product(form, left, right):
    return jnp.einsum(form, left.astype(jnp.float32), right.astype(jnp.float32), precision=lax.Precision.HIGHEST)


def block_probs(head_rows, key_rows, allowed):
    scores = product('igd,cd->igc', head_rows, key_rows) * (head_rows.shape[-1] ** -0.5)
    scores = jnp.where(allowed[:, None, :], scores, -1e30)
    highest = jnp.max(scores, axis=-1, keepdims=True)
    exponent = jnp.exp(scores - highest)
    return exponent / jnp.sum(exponent, axis=-1, keepdims=True)


def pair_pass(pair_queries, pair_kv, prompt_rows, length, head_weight):
    positions = pair_queries.shape[1]
    prompt_span = prompt_rows.shape[0]
    kv_local = pair_kv.shape[2]
    group_size = pair_queries.shape[2] // kv_local
    score_scale = pair_queries.shape[-1] ** -0.5
    prompt_seen = jnp.arange(prompt_span) < length * BLOCK
    causal = jnp.arange(positions)[None, :] <= jnp.arange(positions)[:, None]
    allowed = jnp.concatenate([jnp.broadcast_to(prompt_seen[None, :], (positions, prompt_span)), causal], axis=1)
    blocks = []
    for member in range(2):
        for kv_head in range(kv_local):
            key_rows = jnp.concatenate([prompt_rows[:, kv_head, 0], pair_kv[member, :, kv_head, 0]], axis=0)
            value_rows = jnp.concatenate([prompt_rows[:, kv_head, 1], pair_kv[member, :, kv_head, 1]], axis=0)
            head_rows = pair_queries[member, :, kv_head * group_size:(kv_head + 1) * group_size]
            blocks.append((member, kv_head, head_rows, key_rows, value_rows))
    outputs = {}
    for member, kv_head, head_rows, key_rows, value_rows in blocks:
        weights = block_probs(head_rows, key_rows, allowed)
        rounded = lax.optimization_barrier(weights.astype(jnp.bfloat16))
        outputs[(member, kv_head)] = product('igc,cd->igd', rounded, value_rows).astype(jnp.bfloat16)
    partial_value = jnp.stack([
        jnp.sum(jnp.concatenate([outputs[(member, kv_head)] for kv_head in range(kv_local)], axis=1).astype(jnp.float32) * head_weight[None])
        for member in range(2)]) / positions
    reward = partial_value
    margin = reward[1] - reward[0]
    pair_loss = jnp.logaddexp(0.0, margin)
    sigmoid_gap = jax.nn.sigmoid(margin)
    slopes = (-sigmoid_gap, sigmoid_gap)
    grad_query = [[None] * kv_local for member in range(2)]
    grad_resp = [[None] * kv_local for member in range(2)]
    grad_prompt = [None] * kv_local
    for member, kv_head, head_rows, key_rows, value_rows in blocks:
        weights = block_probs(head_rows, key_rows, allowed)
        rounded = lax.optimization_barrier(weights.astype(jnp.bfloat16))
        head_part = head_weight[kv_head * group_size:(kv_head + 1) * group_size]
        d_out = (loss_scale * slopes[member] / positions * head_part).astype(jnp.bfloat16)
        d_out = jnp.broadcast_to(d_out[None], (positions,) + d_out.shape)
        out_block = outputs[(member, kv_head)]
        d_probs = product('igd,cd->igc', d_out, value_rows)
        row_delta = jnp.sum(d_out.astype(jnp.float32) * out_block.astype(jnp.float32), axis=-1)
        d_scores = lax.optimization_barrier((weights * (d_probs - row_delta[..., None])).astype(jnp.bfloat16))
        grad_query[member][kv_head] = (product('igc,cd->igd', d_scores, key_rows) * score_scale).astype(jnp.bfloat16)
        grad_k = product('igc,igd->cd', d_scores, head_rows) * score_scale
        grad_v = product('igc,igd->cd', rounded, d_out)
        grad_resp[member][kv_head] = jnp.stack([grad_k[prompt_span:], grad_v[prompt_span:]], axis=1).astype(jnp.bfloat16)
        prompt_term = jnp.stack([grad_k[:prompt_span], grad_v[:prompt_span]], axis=1)
        grad_prompt[kv_head] = prompt_term if grad_prompt[kv_head] is None else grad_prompt[kv_head] + prompt_term
    query_out = jnp.stack([jnp.concatenate(grad_query[member], axis=1) for member in range(2)], axis=0)
    resp_out = jnp.stack([jnp.stack(grad_resp[member], axis=1) for member in range(2)], axis=0)
    prompt_out = jnp.stack(grad_prompt, axis=1)
    return pair_loss, query_out, resp_out, prompt_out


def reference(queries, resp_kv, prompt_kv, prompt_of, prompt_len, reward_head):
    def scan_step(running, pair_item):
        pair_queries, pair_kv, prompt_id = pair_item
        length = prompt_len[prompt_id]
        prompt_rows = lax.dynamic_index_in_dim(prompt_kv, prompt_id, 0, keepdims=False)
        pair_loss, query_out, resp_out, prompt_out = pair_pass(pair_queries, pair_kv, prompt_rows, length, reward_head)
        running = running.at[prompt_id].add(prompt_out)
        return running, (pair_loss, query_out, resp_out)

    initial = jnp.zeros(prompt_kv.shape, jnp.float32)
    running, (losses, query_grads, resp_grads) = lax.scan(scan_step, initial, (queries, resp_kv, prompt_of))
    return losses, query_grads, resp_grads, running.astype(jnp.bfloat16)
```

```python
import math

import jax
import jax.numpy as jnp
from jax import lax
from jax.experimental import pallas as pl
from jax.experimental.pallas import tpu as pltpu
from jax.sharding import PartitionSpec as P

BLOCK = 128
TILE = 256

loss_scale = 8192.0


def product(left, right):
    return jnp.dot(left, right, preferred_element_type=jnp.float32)


def product_nt(left, right):
    return lax.dot_general(
        left, right, (((1,), (1,)), ((), ())), preferred_element_type=jnp.float32
    )


def attend_kernel(
    length_ref,
    q_ref,
    kv_ref,
    rkv_ref,
    w_ref,
    gq_ref,
    gp_ref,
    gr_ref,
    reward_ref,
    wrow_ref,
    wt_ref,
    mask_ref,
    mask_t_ref,
    w2_ref,
    kt_ref,
    vt_ref,
    rkt_ref,
    rvt_ref,
    dp_ref,
    drp_ref,
    s_ref,
    p_ref,
    ds_ref,
):
    members, rows, hd = q_ref.shape
    span = kv_ref.shape[0]
    positions = rkv_ref.shape[1]
    heads = w_ref.shape[0]
    blocks = span // BLOCK
    period = wrow_ref.shape[0]
    phases = period // TILE
    tiles = rows // TILE
    wide = 2 * hd
    scale = hd**-0.5
    pace = scale * math.log2(math.e)
    length = length_ref[0]

    for index in range(period // heads):
        wrow_ref[index * heads : (index + 1) * heads, :] = w_ref[...]
    for phase in range(phases):
        part = slice(phase * TILE, (phase + 1) * TILE)
        row = lax.broadcasted_iota(jnp.int32, (TILE, hd), 0) + phase * TILE
        first = (lax.rem(row, heads) < heads // 2).astype(jnp.float32)
        wrow = wrow_ref[part, :]
        mask_ref[part, :] = first.astype(jnp.bfloat16)
        mask_t_ref[:, part] = first.T
        wt_ref[:, part] = wrow.T
        w2 = jnp.concatenate([wrow * first, wrow * (1.0 - first)], axis=1)
        w2_ref[part, :] = w2.astype(jnp.bfloat16)
        w2t = w2.T.astype(jnp.bfloat16)
        dp_ref[:, part] = product(kv_ref[:, wide:], w2t)
        for member in range(members):
            drp_ref[member, :, part] = product(rkv_ref[member, :, wide:], w2t)
    for block in range(blocks):
        part = slice(block * BLOCK, (block + 1) * BLOCK)
        kt_ref[:, part] = kv_ref[part, :wide].astype(jnp.float32).T.astype(jnp.bfloat16)
        vt_ref[:, part] = kv_ref[part, wide:].astype(jnp.float32).T.astype(jnp.bfloat16)
    for member in range(members):
        rkt_ref[member] = rkv_ref[member, :, :wide].astype(jnp.float32).T.astype(jnp.bfloat16)
        rvt_ref[member] = rkv_ref[member, :, wide:].astype(jnp.float32).T.astype(jnp.bfloat16)
    gp_ref[...] = jnp.zeros_like(gp_ref)
    gr_ref[...] = jnp.zeros_like(gr_ref)
    reward_ref[...] = jnp.zeros_like(reward_ref)
    shades = [jnp.where(block < length, 0.0, -1e30) for block in range(blocks)]

    def step(index, carry):
        member = index // tiles
        tile = lax.rem(index, tiles)
        start = pl.multiple_of(tile * TILE, TILE)
        lane = pl.ds(pl.multiple_of(lax.rem(index, phases) * TILE, TILE), TILE)
        q = q_ref[member, pl.ds(start, TILE), :]
        first = mask_ref[lane, :]
        q2 = jnp.concatenate([q * first, q * (1 - first)], axis=1)
        s_ref[:span] = product_nt(kv_ref[:, :wide], q2)
        sr = product_nt(rkv_ref[member, :, :wide], q2)
        causal = (
            lax.broadcasted_iota(jnp.int32, (positions, TILE), 0) * heads
            <= lax.broadcasted_iota(jnp.int32, (positions, TILE), 1) + start
        )
        sr = jnp.where(causal, sr, -1e30)
        highest = jnp.max(sr, axis=0, keepdims=True)
        for block in range(blocks):
            part = slice(block * BLOCK, (block + 1) * BLOCK)
            top = jnp.max(s_ref[part, :], axis=0, keepdims=True) + shades[block]
            highest = jnp.maximum(highest, top)
        er = jnp.exp2((sr - highest) * pace)
        total = jnp.sum(er, axis=0, keepdims=True)
        for block in range(blocks):
            part = slice(block * BLOCK, (block + 1) * BLOCK)
            e = jnp.exp2((s_ref[part, :] - (highest - shades[block])) * pace)
            s_ref[part, :] = e
            total = total + jnp.sum(e, axis=0, keepdims=True)
        inverse = 1.0 / total
        pr = er * inverse
        lr = pr.astype(jnp.bfloat16)
        for block in range(blocks):
            part = slice(block * BLOCK, (block + 1) * BLOCK)
            p = s_ref[part, :] * inverse
            s_ref[part, :] = p
            p_ref[part, :] = p.astype(jnp.bfloat16)
        both = product(vt_ref[...], p_ref[...]) + product(rvt_ref[member], lr)
        first_t = mask_t_ref[:, lane]
        out = jnp.where(first_t > 0.5, both[:hd], both[hd:]).astype(jnp.bfloat16)
        out = out.astype(jnp.float32)
        wt = wt_ref[:, lane]
        reward_ref[pl.ds(member, 1), :] += jnp.sum(out * wt, axis=0, keepdims=True)
        delta = jnp.sum(
            out * wt.astype(jnp.bfloat16).astype(jnp.float32), axis=0, keepdims=True
        )
        for block in range(blocks):
            part = slice(block * BLOCK, (block + 1) * BLOCK)
            ds_ref[part, :] = (s_ref[part, :] * (dp_ref[part, lane] - delta)).astype(jnp.bfloat16)
        dsr = (pr * (drp_ref[member, :, lane] - delta)).astype(jnp.bfloat16)
        both = product(kt_ref[...], ds_ref[...]) + product(rkt_ref[member], dsr)
        gq = jnp.where(first_t > 0.5, both[:hd], both[hd:]) * scale
        gq_ref[member, pl.ds(start, TILE), :] = gq.T
        sign = (2 * member - 1).astype(jnp.float32).astype(jnp.bfloat16)
        w2 = w2_ref[lane, :]
        gr_ref[member, :, :wide] += product(dsr, q2)
        gr_ref[member, :, wide:] += product(lr, w2)
        gp_ref[:, :wide] += product(ds_ref[...], q2 * sign)
        gp_ref[:, wide:] += product(p_ref[...], w2 * sign)
        return carry

    lax.fori_loop(0, members * tiles, step, 0)
    gp_ref[:, :wide] = gp_ref[:, :wide] * scale
    gr_ref[:, :, :wide] = gr_ref[:, :, :wide] * scale


def attend(length, q, kv, rkv, w):
    members, rows, hd = q.shape
    span = kv.shape[0]
    positions = rkv.shape[1]
    heads = w.shape[0]
    period = heads * TILE // math.gcd(heads, TILE)
    wide = 2 * hd
    vmem = pl.BlockSpec(memory_space=pltpu.VMEM)
    return pl.pallas_call(
        attend_kernel,
        out_shape=(
            jax.ShapeDtypeStruct((members, rows, hd), jnp.float32),
            jax.ShapeDtypeStruct((span, 2 * wide), jnp.float32),
            jax.ShapeDtypeStruct((members, positions, 2 * wide), jnp.float32),
            jax.ShapeDtypeStruct((members, TILE), jnp.float32),
        ),
        in_specs=[pl.BlockSpec(memory_space=pltpu.SMEM)] + [vmem] * 4,
        out_specs=(vmem,) * 4,
        scratch_shapes=[
            pltpu.VMEM((period, hd), jnp.float32),
            pltpu.VMEM((hd, period), jnp.float32),
            pltpu.VMEM((period, hd), jnp.bfloat16),
            pltpu.VMEM((hd, period), jnp.float32),
            pltpu.VMEM((period, wide), jnp.bfloat16),
            pltpu.VMEM((wide, span), jnp.bfloat16),
            pltpu.VMEM((wide, span), jnp.bfloat16),
            pltpu.VMEM((members, wide, positions), jnp.bfloat16),
            pltpu.VMEM((members, wide, positions), jnp.bfloat16),
            pltpu.VMEM((span, period), jnp.float32),
            pltpu.VMEM((members, positions, period), jnp.float32),
            pltpu.VMEM((span, TILE), jnp.float32),
            pltpu.VMEM((span, TILE), jnp.bfloat16),
            pltpu.VMEM((span, TILE), jnp.bfloat16),
        ],
        compiler_params=pltpu.CompilerParams(vmem_limit_bytes=48 * 2**20),
    )(length, q, kv, rkv, w)


def pack(kv):
    return jnp.swapaxes(kv, -3, -2).reshape(kv.shape[:-3] + (-1,))


def unpack(flat, kv_heads):
    hd = flat.shape[-1] // (2 * kv_heads)
    return jnp.swapaxes(flat.reshape(flat.shape[:-1] + (2, kv_heads, hd)), -3, -2)


def shards(queries, resp_kv, prompt_kv, prompt_of, prompt_len, reward_head):
    n_resp = lax.axis_size("resp")
    n_prompt = lax.axis_size("prompt")
    pair_index = lax.axis_index(("prompt", "resp"))
    resp_index = lax.axis_index("resp")
    prompt_id = prompt_of[pair_index]
    table = prompt_of.reshape(n_prompt, n_resp)
    column = lax.dynamic_index_in_dim(table, resp_index, 1, keepdims=False)
    length = prompt_len[prompt_id]
    _, members, positions, heads, hd = queries.shape
    kv_heads = prompt_kv.shape[2]

    own = pack(prompt_kv)
    every_prompt = lax.all_gather(own, "resp", axis=0, tiled=True)
    picked = jnp.take(every_prompt, column, axis=0)
    arrived = lax.all_to_all(picked, "prompt", split_axis=0, concat_axis=0, tiled=True)
    whole = arrived.reshape(-1, arrived.shape[-1])

    q = queries.reshape(members, positions * heads, hd)
    gq, gp, gr, reward = attend(length[None], q, whole, pack(resp_kv[0]), reward_head)
    reward = lax.psum(jnp.sum(reward, axis=1), "tensor") / positions
    margin = reward[1] - reward[0]
    pair_loss = jnp.logaddexp(0.0, margin)
    gain = jax.nn.sigmoid(margin) * (loss_scale / positions)
    gains = jnp.stack([-gain, gain])
    query_out = (gq * gains[:, None, None]).astype(jnp.bfloat16).reshape(queries.shape)
    resp_out = unpack((gr * gains[:, None, None]).astype(jnp.bfloat16), kv_heads)[None]

    pieces = (gp * gain).astype(jnp.bfloat16).reshape(arrived.shape)
    returned = lax.all_to_all(pieces, "prompt", split_axis=0, concat_axis=0, tiled=True)
    selector = (column[:, None] == jnp.arange(n_resp)[None, :]).astype(jnp.float32)
    dense = jnp.einsum(
        "pn,prj->nrj",
        selector,
        returned.astype(jnp.float32),
        precision=lax.Precision.HIGHEST,
    )
    owned = lax.psum_scatter(dense.astype(jnp.bfloat16), "resp", scatter_dimension=0, tiled=True)
    return (pair_loss[None], query_out, resp_out, unpack(owned, kv_heads))


def solution(mesh):
    in_specs = (
        P(("prompt", "resp"), None, None, "tensor", None),
        P(("prompt", "resp"), None, None, "tensor", None, None),
        P("resp", "prompt", "tensor", None, None),
        P(),
        P(),
        P("tensor", None),
    )
    out_specs = (
        P(("prompt", "resp")),
        P(("prompt", "resp"), None, None, "tensor", None),
        P(("prompt", "resp"), None, None, "tensor", None, None),
        P("resp", "prompt", "tensor", None, None),
    )
    return jax.shard_map(shards, mesh=mesh, in_specs=in_specs, out_specs=out_specs, check_vma=False)
```

```python
import math

import jax
import jax.numpy as jnp
from jax import lax
from jax.experimental import pallas as pl
from jax.experimental.pallas import tpu as pltpu
from jax.sharding import PartitionSpec as P

BLOCK = 128
TILE = 256

loss_scale = 8192.0


def product(left, right):
    return jnp.dot(left, right, preferred_element_type=jnp.float32)


def product_nt(left, right):
    return lax.dot_general(
        left, right, (((1,), (1,)), ((), ())), preferred_element_type=jnp.float32
    )


def attend_kernel(
    length_ref,
    q_ref,
    kv_ref,
    rkv_ref,
    w_ref,
    gq_ref,
    gp_ref,
    gr_ref,
    reward_ref,
    wrow_ref,
    wt_ref,
    mask_ref,
    mask_t_ref,
    w2_ref,
    kt_ref,
    vt_ref,
    rkt_ref,
    rvt_ref,
    dp_ref,
    drp_ref,
    s_ref,
    p_ref,
    ds_ref,
):
    members, rows, hd = q_ref.shape
    span = kv_ref.shape[0]
    positions = rkv_ref.shape[1]
    heads = w_ref.shape[0]
    blocks = span // BLOCK
    period = wrow_ref.shape[0]
    phases = period // TILE
    tiles = rows // TILE
    wide = 2 * hd
    scale = hd**-0.5
    pace = scale * math.log2(math.e)
    length = length_ref[0]

    for index in range(period // heads):
        wrow_ref[index * heads : (index + 1) * heads, :] = w_ref[...]
    for phase in range(phases):
        part = slice(phase * TILE, (phase + 1) * TILE)
        row = lax.broadcasted_iota(jnp.int32, (TILE, hd), 0) + phase * TILE
        first = (lax.rem(row, heads) < heads // 2).astype(jnp.float32)
        wrow = wrow_ref[part, :]
        mask_ref[part, :] = first.astype(jnp.bfloat16)
        mask_t_ref[:, part] = first.T
        wt_ref[:, part] = wrow.T
        w2 = jnp.concatenate([wrow * first, wrow * (1.0 - first)], axis=1)
        w2_ref[part, :] = w2.astype(jnp.bfloat16)
        w2t = w2.T.astype(jnp.bfloat16)
        dp_ref[:, part] = product(kv_ref[:, wide:], w2t)
        for member in range(members):
            drp_ref[member, :, part] = product(rkv_ref[member, :, wide:], w2t)
    for block in range(blocks):
        part = slice(block * BLOCK, (block + 1) * BLOCK)
        kt_ref[:, part] = kv_ref[part, :wide].astype(jnp.float32).T.astype(jnp.bfloat16)
        vt_ref[:, part] = kv_ref[part, wide:].astype(jnp.float32).T.astype(jnp.bfloat16)
    for member in range(members):
        rkt_ref[member] = rkv_ref[member, :, :wide].astype(jnp.float32).T.astype(jnp.bfloat16)
        rvt_ref[member] = rkv_ref[member, :, wide:].astype(jnp.float32).T.astype(jnp.bfloat16)
    gp_ref[...] = jnp.zeros_like(gp_ref)
    gr_ref[...] = jnp.zeros_like(gr_ref)
    reward_ref[...] = jnp.zeros_like(reward_ref)
    shades = [jnp.where(block < length, 0.0, -1e30) for block in range(blocks)]

    def step(index, carry):
        member = index // tiles
        tile = lax.rem(index, tiles)
        start = pl.multiple_of(tile * TILE, TILE)
        lane = pl.ds(pl.multiple_of(lax.rem(index, phases) * TILE, TILE), TILE)
        q = q_ref[member, pl.ds(start, TILE), :]
        first = mask_ref[lane, :]
        q2 = jnp.concatenate([q * first, q * (1 - first)], axis=1)
        s_ref[:span] = product_nt(kv_ref[:, :wide], q2)
        sr = product_nt(rkv_ref[member, :, :wide], q2)
        causal = (
            lax.broadcasted_iota(jnp.int32, (positions, TILE), 0) * heads
            <= lax.broadcasted_iota(jnp.int32, (positions, TILE), 1) + start
        )
        sr = jnp.where(causal, sr, -1e30)
        highest = jnp.max(sr, axis=0, keepdims=True)
        for block in range(blocks):
            part = slice(block * BLOCK, (block + 1) * BLOCK)
            top = jnp.max(s_ref[part, :], axis=0, keepdims=True) + shades[block]
            highest = jnp.maximum(highest, top)
        er = jnp.exp2((sr - highest) * pace)
        total = jnp.sum(er, axis=0, keepdims=True)
        for block in range(blocks):
            part = slice(block * BLOCK, (block + 1) * BLOCK)
            e = jnp.exp2((s_ref[part, :] - (highest - shades[block])) * pace)
            s_ref[part, :] = e
            total = total + jnp.sum(e, axis=0, keepdims=True)
        inverse = 1.0 / total
        pr = er * inverse
        lr = pr.astype(jnp.bfloat16)
        for block in range(blocks):
            part = slice(block * BLOCK, (block + 1) * BLOCK)
            p = s_ref[part, :] * inverse
            s_ref[part, :] = p
            p_ref[part, :] = p.astype(jnp.bfloat16)
        both = product(vt_ref[...], p_ref[...]) + product(rvt_ref[member], lr)
        first_t = mask_t_ref[:, lane]
        out = jnp.where(first_t > 0.5, both[:hd], both[hd:]).astype(jnp.bfloat16)
        out = out.astype(jnp.float32)
        wt = wt_ref[:, lane]
        reward_ref[pl.ds(member, 1), :] += jnp.sum(out * wt, axis=0, keepdims=True)
        delta = jnp.sum(
            out * wt.astype(jnp.bfloat16).astype(jnp.float32), axis=0, keepdims=True
        )
        for block in range(blocks):
            part = slice(block * BLOCK, (block + 1) * BLOCK)
            ds_ref[part, :] = (s_ref[part, :] * (dp_ref[part, lane] - delta)).astype(jnp.bfloat16)
        dsr = (pr * (drp_ref[member, :, lane] - delta)).astype(jnp.bfloat16)
        both = product(kt_ref[...], ds_ref[...]) + product(rkt_ref[member], dsr)
        gq = jnp.where(first_t > 0.5, both[:hd], both[hd:]) * scale
        gq_ref[member, pl.ds(start, TILE), :] = gq.T
        sign = (2 * member - 1).astype(jnp.float32).astype(jnp.bfloat16)
        w2 = w2_ref[lane, :]
        gr_ref[member, :, :wide] += product(dsr, q2)
        gr_ref[member, :, wide:] += product(lr, w2)
        gp_ref[:, :wide] += product(ds_ref[...], q2 * sign)
        gp_ref[:, wide:] += product(p_ref[...], w2 * sign)
        return carry

    lax.fori_loop(0, members * tiles, step, 0)
    gp_ref[:, :wide] = gp_ref[:, :wide] * scale
    gr_ref[:, :, :wide] = gr_ref[:, :, :wide] * scale


def attend(length, q, kv, rkv, w):
    members, rows, hd = q.shape
    span = kv.shape[0]
    positions = rkv.shape[1]
    heads = w.shape[0]
    period = heads * TILE // math.gcd(heads, TILE)
    wide = 2 * hd
    vmem = pl.BlockSpec(memory_space=pltpu.VMEM)
    return pl.pallas_call(
        attend_kernel,
        out_shape=(
            jax.ShapeDtypeStruct((members, rows, hd), jnp.float32),
            jax.ShapeDtypeStruct((span, 2 * wide), jnp.float32),
            jax.ShapeDtypeStruct((members, positions, 2 * wide), jnp.float32),
            jax.ShapeDtypeStruct((members, TILE), jnp.float32),
        ),
        in_specs=[pl.BlockSpec(memory_space=pltpu.SMEM)] + [vmem] * 4,
        out_specs=(vmem,) * 4,
        scratch_shapes=[
            pltpu.VMEM((period, hd), jnp.float32),
            pltpu.VMEM((hd, period), jnp.float32),
            pltpu.VMEM((period, hd), jnp.bfloat16),
            pltpu.VMEM((hd, period), jnp.float32),
            pltpu.VMEM((period, wide), jnp.bfloat16),
            pltpu.VMEM((wide, span), jnp.bfloat16),
            pltpu.VMEM((wide, span), jnp.bfloat16),
            pltpu.VMEM((members, wide, positions), jnp.bfloat16),
            pltpu.VMEM((members, wide, positions), jnp.bfloat16),
            pltpu.VMEM((span, period), jnp.float32),
            pltpu.VMEM((members, positions, period), jnp.float32),
            pltpu.VMEM((span, TILE), jnp.float32),
            pltpu.VMEM((span, TILE), jnp.bfloat16),
            pltpu.VMEM((span, TILE), jnp.bfloat16),
        ],
        compiler_params=pltpu.CompilerParams(vmem_limit_bytes=48 * 2**20),
    )(length, q, kv, rkv, w)


LONG = 4
WIDE = 4
MESH = pl.DeviceIdType.MESH


class Place:
    def __init__(self):
        prompt = lax.axis_index("prompt")
        resp = lax.axis_index("resp")
        self.core = lax.rem(prompt, 2)
        self.low = lax.div(prompt, 2)
        self.high = lax.div(resp, WIDE)
        self.x = lax.rem(resp, WIDE)
        self.tensor = lax.axis_index("tensor")
        self.z = self.high * LONG + self.low

    def at(self, dz, dx, core):
        ring = LONG * LONG
        z = lax.rem(self.z + dz + ring, ring)
        x = lax.rem(self.x + dx + WIDE, WIDE)
        return (lax.rem(z, LONG) * 2 + core, lax.div(z, LONG) * WIDE + x, self.tensor)

    def block(self, dz, core):
        return lax.rem(self.low + dz + LONG, LONG) * 2 + core


def remote(src, dst, send, recv, target):
    return pltpu.make_async_remote_copy(
        src_ref=src,
        dst_ref=dst,
        send_sem=send,
        recv_sem=recv,
        device_id=target,
        device_id_type=MESH,
    )


def greet(senders):
    barrier = pltpu.get_barrier_semaphore()
    for device in senders:
        pl.semaphore_signal(barrier, inc=1, device_id=device, device_id_type=MESH)
    pl.semaphore_wait(barrier, len(senders))


def gather_kernel(prompt_of_ref, own_ref, whole_ref, all_ref, out_ref, z_send, z_recv, x_send, x_recv, c_send, c_recv):
    me = Place()
    core = me.core
    rows = own_ref.shape[0]
    half = rows // 2
    parts = (pl.ds(0, half), pl.ds(half, half))
    up, down = me.at(LONG, 0, core), me.at(-LONG, 0, core)
    right, left = me.at(0, 1, core), me.at(0, -1, core)
    greet(
        [up, down, right, left, me.at(0, 0, 1 - core), me.at(-2, 0, 0), me.at(2, 0, 1)]
        + [me.at(dz, 0, c) for dz in (1, -1) for c in range(2)]
    )

    def slot(dzh, dx):
        return lax.rem(me.high + dzh + LONG, LONG) * WIDE + lax.rem(me.x + dx + WIDE, WIDE)

    sent = []

    def push(ref, sends, recvs, index, target):
        copy = remote(ref, ref, sends.at[index], recvs.at[index], target)
        copy.start()
        sent.append(copy)

    def await_copy(ref, recvs, index):
        remote(ref, ref, z_send.at[0], recvs.at[index], up).wait_recv()

    def spread(order, dzh):
        block = all_ref.at[slot(dzh, 0)]
        push(block, x_send, x_recv, 4 * order, right)
        push(block, x_send, x_recv, 4 * order + 1, left)

    def relay(order, dzh):
        block = all_ref.at[slot(dzh, -1)]
        await_copy(block, x_recv, 4 * order)
        push(block.at[parts[0]], x_send, x_recv, 4 * order + 2, right)
        block = all_ref.at[slot(dzh, 1)]
        await_copy(block, x_recv, 4 * order + 1)
        push(block.at[parts[1]], x_send, x_recv, 4 * order + 3, left)

    all_ref[slot(0, 0)] = own_ref[...]
    block = all_ref.at[slot(0, 0)]
    push(block, z_send, z_recv, 0, up)
    push(block, z_send, z_recv, 1, down)
    spread(0, 0)
    block = all_ref.at[slot(-1, 0)]
    await_copy(block, z_recv, 0)
    push(block.at[parts[0]], z_send, z_recv, 2, up)
    block = all_ref.at[slot(1, 0)]
    await_copy(block, z_recv, 1)
    push(block.at[parts[1]], z_send, z_recv, 3, down)
    spread(1, -1)
    spread(2, 1)
    relay(0, 0)
    block = all_ref.at[slot(2, 0)]
    await_copy(block.at[parts[0]], z_recv, 2)
    await_copy(block.at[parts[1]], z_recv, 3)
    spread(3, 2)
    for order, dzh in ((1, -1), (2, 1), (3, 2)):
        relay(order, dzh)
    for order, dzh in ((0, 0), (1, -1), (2, 1), (3, 2)):
        block = all_ref.at[slot(dzh, 2)]
        await_copy(block.at[parts[0]], x_recv, 4 * order + 2)
        await_copy(block.at[parts[1]], x_recv, 4 * order + 3)

    here = whole_ref.at[pl.ds(me.block(0, core) * rows, rows)]
    n_resp = LONG * WIDE

    def wanted(device):
        return all_ref[prompt_of_ref[device[0] * n_resp + device[1]]]

    far = 2 - 4 * core
    index = 0
    for kind, dz in ((3, far), (1, 1), (2, -1), (0, 0)):
        for c in range(2) if kind else (1 - core,):
            target = me.at(dz, 0, c)
            out_ref[index] = wanted(target)
            copy = remote(out_ref.at[index], here, c_send.at[index], c_recv.at[2 * kind + core], target)
            copy.start()
            sent.append(copy)
            index += 1
    here[...] = wanted(me.at(0, 0, core))
    for kind, dz in ((0, 0), (1, -1), (2, 1), (3, 2)):
        for c in range(2) if kind else (1 - core,):
            block = whole_ref.at[pl.ds(me.block(dz, c) * rows, rows)]
            remote(block, block, c_send.at[0], c_recv.at[2 * kind + c], up).wait_recv()
    for copy in sent:
        copy.wait_send()


def gather(prompt_of, own):
    rows, width = own.shape
    n_prompt, n_resp = 2 * LONG, LONG * WIDE
    vmem = pl.BlockSpec(memory_space=pltpu.VMEM)
    dma = pltpu.SemaphoreType.DMA
    return pl.pallas_call(
        gather_kernel,
        out_shape=jax.ShapeDtypeStruct((n_prompt * rows, width), own.dtype),
        in_specs=[pl.BlockSpec(memory_space=pltpu.SMEM), vmem],
        out_specs=vmem,
        scratch_shapes=[
            pltpu.VMEM((n_resp, rows, width), own.dtype),
            pltpu.VMEM((n_prompt - 1, rows, width), own.dtype),
            dma((4,)),
            dma((4,)),
            dma((16,)),
            dma((16,)),
            dma((n_prompt,)),
            dma((n_prompt,)),
        ],
        compiler_params=pltpu.CompilerParams(
            collective_id=0, has_side_effects=True, vmem_limit_bytes=32 * 2**20
        ),
    )(prompt_of, own)


def scatter_kernel(prompt_of_ref, piece_ref, owned_ref, got_ref, dense_ref, sum_ref, x1_ref, x2_ref, z1_ref, z2_ref, z_send, z_recv, x_send, x_recv, c_send, c_recv):
    me = Place()
    core = me.core
    rows, width = owned_ref.shape
    half = rows // 2
    parts = (pl.ds(0, half), pl.ds(half, half))
    up, down = me.at(LONG, 0, core), me.at(-LONG, 0, core)
    right, left = me.at(0, 1, core), me.at(0, -1, core)
    far = 2 - 4 * core
    n_resp = LONG * WIDE
    greet(
        [up, down, right, left, me.at(0, 0, 1 - core)]
        + [me.at(dz, 0, c) for dz in (1, -1, far) for c in range(2)]
    )

    def add(left_ref, right_ref):
        return left_ref[...].astype(jnp.float32) + right_ref[...].astype(jnp.float32)

    sent = []

    def push(src, dst, sends, recvs, index, landing, target):
        copy = remote(src, dst, sends.at[index], recvs.at[landing], target)
        copy.start()
        sent.append(copy)

    def await_copy(ref, recvs, index):
        remote(ref, ref, z_send.at[0], recvs.at[index], up).wait_recv()

    index = 0
    for kind, dz in ((3, 2), (1, 1), (2, -1), (0, 0)):
        for c in range(2) if kind else (1 - core,):
            block = piece_ref.at[pl.ds(me.block(dz, c) * rows, rows)]
            target = me.at(dz if kind != 3 else 4 * c - 2, 0, c)
            push(block, got_ref.at[2 * kind + core], c_send, c_recv, index, 2 * kind + core, target)
            index += 1
    got_ref[core] = piece_ref[pl.ds(me.block(0, core) * rows, rows), :]
    names = []
    for kind, dz in ((0, 0), (1, -1), (2, 1), (3, far)):
        for c in range(2):
            device = me.at(dz, 0, c)
            names.append(prompt_of_ref[device[0] * n_resp + device[1]])
    for kind in range(4):
        for c in range(2) if kind else (1 - core,):
            await_copy(got_ref.at[2 * kind + c], c_recv, 2 * kind + c)

    chunk = 16
    strip = 128
    for order, dzh in enumerate((2, 1, 3, 0)):
        base = lax.rem(me.high + dzh, LONG) * WIDE
        for dx in (2, 1, 3, 0):
            prompt = base + lax.rem(me.x + dx, WIDE)
            picks = [jnp.where(name == prompt, 1.0, 0.0) for name in names]

            def select(index, carry):
                row = pl.ds(pl.multiple_of(index * chunk, chunk), chunk)
                for start in range(0, width, strip):
                    column = slice(start, start + strip)
                    total = picks[0] * got_ref[0, row, column].astype(jnp.float32)
                    for source in range(1, len(names)):
                        total += picks[source] * got_ref[source, row, column].astype(jnp.float32)
                    dense_ref[dzh, dx, row, column] = total.astype(dense_ref.dtype)
                return carry

            lax.fori_loop(0, rows // chunk, select, 0)
            if dx == 2:
                block = dense_ref.at[dzh, dx]
                push(block.at[parts[0]], x1_ref.at[0, dzh], x_send, x_recv, 4 * order, 4 * order, right)
                push(block.at[parts[1]], x1_ref.at[1, dzh], x_send, x_recv, 4 * order + 1, 4 * order + 1, left)

    def x_turn(order, dzh):
        for side, (dx, target) in enumerate(((1, right), (3, left))):
            landed = x1_ref.at[side, dzh]
            await_copy(landed, x_recv, 4 * order + side)
            block = dense_ref.at[dzh, dx]
            section = block.at[parts[side]]
            section[...] = add(section, landed).astype(section.dtype)
            push(block, x2_ref.at[side, dzh], x_send, x_recv, 4 * order + 2 + side, 4 * order + 2 + side, target)

    def x_end(order, dzh):
        for side in range(2):
            await_copy(x2_ref.at[side, dzh], x_recv, 4 * order + 2 + side)
        total = add(x2_ref.at[0, dzh], x2_ref.at[1, dzh])
        sum_ref[dzh] = (total + dense_ref[dzh, 0].astype(jnp.float32)).astype(sum_ref.dtype)

    def z_turn(side, dzh, target):
        landed = z1_ref.at[side]
        await_copy(landed, z_recv, side)
        block = sum_ref.at[dzh]
        section = block.at[parts[side]]
        section[...] = add(section, landed).astype(section.dtype)
        push(block, z2_ref.at[side], z_send, z_recv, 2 + side, 2 + side, target)

    x_turn(0, 2)
    x_turn(1, 1)
    x_turn(2, 3)
    x_turn(3, 0)
    x_end(0, 2)
    push(sum_ref.at[2, parts[0]], z1_ref.at[0], z_send, z_recv, 0, 0, up)
    push(sum_ref.at[2, parts[1]], z1_ref.at[1], z_send, z_recv, 1, 1, down)
    x_end(1, 1)
    z_turn(0, 1, up)
    x_end(2, 3)
    z_turn(1, 3, down)
    x_end(3, 0)
    for side in range(2):
        await_copy(z2_ref.at[side], z_recv, 2 + side)
    total = add(z2_ref.at[0], z2_ref.at[1]) + sum_ref[0].astype(jnp.float32)
    owned_ref[...] = total.astype(owned_ref.dtype)
    for copy in sent:
        copy.wait_send()


def scatter(prompt_of, pieces):
    n_prompt, n_resp = 2 * LONG, LONG * WIDE
    rows, width = pieces.shape[0] // n_prompt, pieces.shape[1]
    vmem = pl.BlockSpec(memory_space=pltpu.VMEM)
    dma = pltpu.SemaphoreType.DMA
    dtype = pieces.dtype
    return pl.pallas_call(
        scatter_kernel,
        out_shape=jax.ShapeDtypeStruct((rows, width), dtype),
        in_specs=[pl.BlockSpec(memory_space=pltpu.SMEM), vmem],
        out_specs=vmem,
        scratch_shapes=[
            pltpu.VMEM((n_prompt, rows, width), dtype),
            pltpu.VMEM((LONG, WIDE, rows, width), dtype),
            pltpu.VMEM((LONG, rows, width), dtype),
            pltpu.VMEM((2, LONG, rows // 2, width), dtype),
            pltpu.VMEM((2, LONG, rows, width), dtype),
            pltpu.VMEM((2, rows // 2, width), dtype),
            pltpu.VMEM((2, rows, width), dtype),
            dma((4,)),
            dma((4,)),
            dma((16,)),
            dma((16,)),
            dma((n_prompt,)),
            dma((n_prompt,)),
        ],
        compiler_params=pltpu.CompilerParams(
            collective_id=1, has_side_effects=True, vmem_limit_bytes=32 * 2**20
        ),
    )(prompt_of, pieces)


def pack(kv):
    return jnp.swapaxes(kv, -3, -2).reshape(kv.shape[:-3] + (-1,))


def unpack(flat, kv_heads):
    hd = flat.shape[-1] // (2 * kv_heads)
    return jnp.swapaxes(flat.reshape(flat.shape[:-1] + (2, kv_heads, hd)), -3, -2)


def shards(queries, resp_kv, prompt_kv, prompt_of, prompt_len, reward_head):
    pair_index = lax.axis_index(("prompt", "resp"))
    length = prompt_len[prompt_of[pair_index]]
    _, members, positions, heads, hd = queries.shape
    kv_heads = prompt_kv.shape[2]

    whole = gather(prompt_of, pack(prompt_kv[0]))

    q = queries.reshape(members, positions * heads, hd)
    gq, gp, gr, reward = attend(length[None], q, whole, pack(resp_kv[0]), reward_head)
    reward = lax.psum(jnp.sum(reward, axis=1), "tensor") / positions
    margin = reward[1] - reward[0]
    pair_loss = jnp.logaddexp(0.0, margin)
    gain = jax.nn.sigmoid(margin) * (loss_scale / positions)
    gains = jnp.stack([-gain, gain])
    query_out = (gq * gains[:, None, None]).astype(jnp.bfloat16).reshape(queries.shape)
    resp_out = unpack((gr * gains[:, None, None]).astype(jnp.bfloat16), kv_heads)[None]

    owned = scatter(prompt_of, (gp * gain).astype(jnp.bfloat16))
    return (pair_loss[None], query_out, resp_out, unpack(owned, kv_heads)[None])


def solution(mesh):
    in_specs = (
        P(("prompt", "resp"), None, None, "tensor", None),
        P(("prompt", "resp"), None, None, "tensor", None, None),
        P("resp", "prompt", "tensor", None, None),
        P(),
        P(),
        P("tensor", None),
    )
    out_specs = (
        P(("prompt", "resp")),
        P(("prompt", "resp"), None, None, "tensor", None),
        P(("prompt", "resp"), None, None, "tensor", None, None),
        P("resp", "prompt", "tensor", None, None),
    )
    return jax.shard_map(shards, mesh=mesh, in_specs=in_specs, out_specs=out_specs, check_vma=False)
```

```python
import math

import jax
import jax.numpy as jnp
from jax import lax
from jax.experimental import pallas as pl
from jax.experimental.pallas import tpu as pltpu
from jax.sharding import PartitionSpec as P

BLOCK = 128
TILE = 256

loss_scale = 8192.0


def product(left, right):
    return jnp.dot(left, right, preferred_element_type=jnp.float32)


def product_nt(left, right):
    return lax.dot_general(
        left, right, (((1,), (1,)), ((), ())), preferred_element_type=jnp.float32
    )


LONG = 4
WIDE = 4
MESH = pl.DeviceIdType.MESH


class Place:
    def __init__(self):
        prompt = lax.axis_index("prompt")
        resp = lax.axis_index("resp")
        self.core = lax.rem(prompt, 2)
        self.low = lax.div(prompt, 2)
        self.high = lax.div(resp, WIDE)
        self.x = lax.rem(resp, WIDE)
        self.tensor = lax.axis_index("tensor")
        self.z = self.high * LONG + self.low

    def at(self, dz, dx, core):
        ring = LONG * LONG
        z = lax.rem(self.z + dz + ring, ring)
        x = lax.rem(self.x + dx + WIDE, WIDE)
        return (lax.rem(z, LONG) * 2 + core, lax.div(z, LONG) * WIDE + x, self.tensor)

    def block(self, dz, core):
        return lax.rem(self.low + dz + LONG, LONG) * 2 + core


def remote(src, dst, send, recv, target):
    return pltpu.make_async_remote_copy(
        src_ref=src,
        dst_ref=dst,
        send_sem=send,
        recv_sem=recv,
        device_id=target,
        device_id_type=MESH,
    )


def pair_kernel(
    prompt_of_ref,
    prompt_len_ref,
    q_ref,
    own_ref,
    rkv_ref,
    w_ref,
    gq_ref,
    gr_ref,
    owned_ref,
    margin_ref,
    all_k_ref,
    all_v_ref,
    out_ref,
    whole_ref,
    wrow_ref,
    wt_ref,
    mask_ref,
    mask_t_ref,
    w2_ref,
    w2t_ref,
    kt_ref,
    vt_ref,
    rkt_ref,
    rvt_ref,
    dp_ref,
    drp_ref,
    p_ref,
    pr_ref,
    low_ref,
    delta_ref,
    reward_ref,
    gqf_ref,
    gpf_ref,
    grf_ref,
    vote_ref,
    piece_ref,
    got_ref,
    dense_ref,
    sum_ref,
    x1_ref,
    x2_ref,
    z1_ref,
    z2_ref,
    z_send,
    z_recv,
    x_send,
    x_recv,
    c_send,
    c_recv,
    y_send,
    y_recv,
    zb_send,
    zb_recv,
    xb_send,
    xb_recv,
    cb_send,
    cb_recv,
):
    members, rows, hd = q_ref.shape
    block_rows = own_ref.shape[1]
    span = whole_ref.shape[1]
    positions = rkv_ref.shape[2]
    heads = w_ref.shape[0]
    blocks = span // BLOCK
    period = wrow_ref.shape[0]
    phases = period // TILE
    tiles = rows // TILE
    wide = 2 * hd
    scale = hd**-0.5
    pace = scale * math.log2(math.e)
    n_resp = LONG * WIDE
    n_tensor = vote_ref.shape[0]

    me = Place()
    core = me.core
    half = block_rows // 2
    parts = (pl.ds(0, half), pl.ds(half, half))
    up, down = me.at(LONG, 0, core), me.at(-LONG, 0, core)
    right, left = me.at(0, 1, core), me.at(0, -1, core)
    far = 2 - 4 * core
    here = me.at(0, 0, core)
    peers = [
        (here[0], here[1], lax.rem(me.tensor + step, n_tensor)) for step in range(1, n_tensor)
    ]
    barrier = pltpu.get_barrier_semaphore()
    friends = (
        [up, down, right, left, me.at(0, 0, 1 - core)]
        + [me.at(dz, 0, c) for dz in (1, -1) for c in range(2)]
        + [me.at(-2, 0, 0), me.at(2, 0, 1), me.at(far, 0, core)]
        + peers
    )
    for device in friends:
        pl.semaphore_signal(barrier, inc=1, device_id=device, device_id_type=MESH)
    pl.semaphore_wait(barrier, len(friends))

    sent = []

    def push(src, dst, send, recv, target):
        copy = remote(src, dst, send, recv, target)
        copy.start()
        sent.append(copy)

    def landed(ref, recv):
        remote(ref, ref, y_send.at[0], recv, up).wait_recv()

    def slot(dzh, dx):
        return lax.rem(me.high + dzh + LONG, LONG) * WIDE + lax.rem(me.x + dx + WIDE, WIDE)

    tables = (all_k_ref, all_v_ref)

    def spread(part, order, dzh):
        block = tables[part].at[slot(dzh, 0)]
        for side, target in enumerate((right, left)):
            index = 4 * order + side
            push(block, block, x_send.at[part, index], x_recv.at[part, index], target)

    def relay(part, order, dzh):
        for side, (dx, target) in enumerate(((-1, right), (1, left))):
            block = tables[part].at[slot(dzh, dx)]
            landed(block, x_recv.at[part, 4 * order + side])
            section = block.at[parts[side]]
            index = 4 * order + 2 + side
            push(section, section, x_send.at[part, index], x_recv.at[part, index], target)

    def begin(part):
        tables[part][slot(0, 0)] = own_ref[part]
        block = tables[part].at[slot(0, 0)]
        push(block, block, z_send.at[part, 0], z_recv.at[part, 0], up)
        push(block, block, z_send.at[part, 1], z_recv.at[part, 1], down)
        spread(part, 0, 0)

    def turn(part):
        for side, (dzh, target) in enumerate(((-1, up), (1, down))):
            block = tables[part].at[slot(dzh, 0)]
            landed(block, z_recv.at[part, side])
            section = block.at[parts[side]]
            push(section, section, z_send.at[part, 2 + side], z_recv.at[part, 2 + side], target)

    def finish(part):
        spread(part, 1, -1)
        spread(part, 2, 1)
        relay(part, 0, 0)
        block = tables[part].at[slot(2, 0)]
        for side in range(2):
            landed(block.at[parts[side]], z_recv.at[part, 2 + side])
        spread(part, 3, 2)
        for order, dzh in ((1, -1), (2, 1), (3, 2)):
            relay(part, order, dzh)
        for order, dzh in ((0, 0), (1, -1), (2, 1), (3, 2)):
            block = tables[part].at[slot(dzh, 2)]
            for side in range(2):
                landed(block.at[parts[side]], x_recv.at[part, 4 * order + 2 + side])

    def place(device_block):
        return pl.ds(pl.multiple_of(device_block * block_rows, block_rows), block_rows)

    def name(device):
        return prompt_of_ref[device[0] * n_resp + device[1]]

    def deliver(part):
        mine = whole_ref.at[part, place(me.block(0, core))]
        index = 0
        for kind, dz in ((3, far), (1, 1), (2, -1), (0, 0)):
            for c in range(2) if kind else (1 - core,):
                target = me.at(dz, 0, c)
                out_ref[part, index] = tables[part][name(target)]
                push(
                    out_ref.at[part, index],
                    mine,
                    c_send.at[part, index],
                    c_recv.at[part, 2 * kind + core],
                    target,
                )
                index += 1
        mine[...] = tables[part][name(here)]

    def receive(part):
        for kind, dz in ((0, 0), (1, -1), (2, 1), (3, 2)):
            for c in range(2) if kind else (1 - core,):
                landed(whole_ref.at[part, place(me.block(dz, c))], c_recv.at[part, 2 * kind + c])

    begin(0)

    for index in range(period // heads):
        wrow_ref[index * heads : (index + 1) * heads, :] = w_ref[...]
    for phase in range(phases):
        part = slice(phase * TILE, (phase + 1) * TILE)
        row = lax.broadcasted_iota(jnp.int32, (TILE, hd), 0) + phase * TILE
        first = (lax.rem(row, heads) < heads // 2).astype(jnp.float32)
        wrow = wrow_ref[part, :]
        mask_ref[part, :] = first.astype(jnp.bfloat16)
        mask_t_ref[:, part] = first.T
        wt_ref[:, part] = wrow.T
        w2 = jnp.concatenate([wrow * first, wrow * (1.0 - first)], axis=1)
        w2_ref[part, :] = w2.astype(jnp.bfloat16)
        w2t_ref[:, part] = w2.T.astype(jnp.bfloat16)
    for member in range(members):
        rkt_ref[member] = rkv_ref[member, 0].astype(jnp.float32).T.astype(jnp.bfloat16)
        rvt_ref[member] = rkv_ref[member, 1].astype(jnp.float32).T.astype(jnp.bfloat16)
        drp_ref[member] = product(rkv_ref[member, 1], w2t_ref[...])
    gpf_ref[...] = jnp.zeros_like(gpf_ref)
    grf_ref[...] = jnp.zeros_like(grf_ref)
    reward_ref[...] = jnp.zeros_like(reward_ref)

    turn(0)
    begin(1)
    finish(0)
    deliver(0)
    turn(1)
    finish(1)
    deliver(1)

    length = prompt_len_ref[name(here)]
    shades = [jnp.where(block < length, 0.0, -1e30) for block in range(blocks)]
    strips = [slice(block * BLOCK, (block + 1) * BLOCK) for block in range(blocks)]

    def where_is(index):
        member = lax.div(index, tiles)
        start = pl.multiple_of(lax.rem(index, tiles) * TILE, TILE)
        lane = pl.ds(pl.multiple_of(lax.rem(index, phases) * TILE, TILE), TILE)
        sign = (2 * member - 1).astype(jnp.float32).astype(jnp.bfloat16)
        return member, start, lane, sign

    def stacked(member, start, lane):
        q = q_ref[member, pl.ds(start, TILE), :]
        first = mask_ref[lane, :]
        return jnp.concatenate([q * first, q * (1 - first)], axis=1)

    def score_step(index, carry):
        member, start, lane, sign = where_is(index)
        q2 = stacked(member, start, lane)
        p_ref[index] = product_nt(whole_ref[0], q2)
        sr = product_nt(rkv_ref[member, 0], q2)
        causal = (
            lax.broadcasted_iota(jnp.int32, (positions, TILE), 0) * heads
            <= lax.broadcasted_iota(jnp.int32, (positions, TILE), 1) + start
        )
        sr = jnp.where(causal, sr, -1e30)
        highest = jnp.max(sr, axis=0, keepdims=True)
        for strip, shade in zip(strips, shades):
            top = jnp.max(p_ref[index, strip, :], axis=0, keepdims=True) + shade
            highest = jnp.maximum(highest, top)
        er = jnp.exp2((sr - highest) * pace)
        total = jnp.sum(er, axis=0, keepdims=True)
        for strip, shade in zip(strips, shades):
            e = jnp.exp2((p_ref[index, strip, :] - (highest - shade)) * pace)
            p_ref[index, strip, :] = e
            total = total + jnp.sum(e, axis=0, keepdims=True)
        inverse = 1.0 / total
        pr = er * inverse
        pr_ref[index] = pr
        for strip in strips:
            p = p_ref[index, strip, :] * inverse
            p_ref[index, strip, :] = p
            low_ref[index, strip, :] = p.astype(jnp.bfloat16)
        w2 = w2_ref[lane, :]
        grf_ref[member, 1] += product(pr.astype(jnp.bfloat16), w2)
        gpf_ref[1] += product(low_ref[index], w2 * sign)
        return carry

    def out_step(index, carry):
        member, start, lane, sign = where_is(index)
        both = product(vt_ref[...], low_ref[index])
        both += product(rvt_ref[member], pr_ref[index].astype(jnp.bfloat16))
        out = jnp.where(mask_t_ref[:, lane] > 0.5, both[:hd], both[hd:]).astype(jnp.bfloat16)
        out = out.astype(jnp.float32)
        wt = wt_ref[:, lane]
        reward_ref[pl.ds(member, 1), :] += jnp.sum(out * wt, axis=0, keepdims=True)
        delta_ref[pl.ds(index, 1), :] = jnp.sum(
            out * wt.astype(jnp.bfloat16).astype(jnp.float32), axis=0, keepdims=True
        )
        return carry

    def back_step(index, carry):
        member, start, lane, sign = where_is(index)
        q2 = stacked(member, start, lane)
        delta = delta_ref[pl.ds(index, 1), :]
        for strip in strips:
            low_ref[index, strip, :] = (
                p_ref[index, strip, :] * (dp_ref[strip, lane] - delta)
            ).astype(jnp.bfloat16)
        dsr = (pr_ref[index] * (drp_ref[member, :, lane] - delta)).astype(jnp.bfloat16)
        both = product(kt_ref[...], low_ref[index]) + product(rkt_ref[member], dsr)
        gq = jnp.where(mask_t_ref[:, lane] > 0.5, both[:hd], both[hd:]) * scale
        gqf_ref[member, pl.ds(start, TILE), :] = gq.T
        grf_ref[member, 0] += product(dsr, q2)
        gpf_ref[0] += product(low_ref[index], q2 * sign)
        return carry

    count = members * tiles
    receive(0)
    for strip in strips:
        kt_ref[:, strip] = whole_ref[0, strip, :].astype(jnp.float32).T.astype(jnp.bfloat16)
    lax.fori_loop(0, count, score_step, 0)
    receive(1)
    for strip in strips:
        vt_ref[:, strip] = whole_ref[1, strip, :].astype(jnp.float32).T.astype(jnp.bfloat16)
    lax.fori_loop(0, count, out_step, 0)

    ballot = vote_ref.at[me.tensor]
    for member in range(members):
        total = jnp.sum(reward_ref[member : member + 1, :], axis=1, keepdims=True)
        ballot[8 * member : 8 * (member + 1), :] = jnp.broadcast_to(total, (8, hd))
    for step, target in enumerate(peers):
        push(ballot, ballot, y_send.at[step], y_recv.at[step], target)
    dp_ref[...] = product(whole_ref[1], w2t_ref[...])
    lax.fori_loop(0, count // 2, back_step, 0)

    for step in range(1, n_tensor):
        source = lax.rem(me.tensor + n_tensor - step, n_tensor)
        landed(vote_ref.at[source], y_recv.at[step - 1])
    reward = vote_ref[0]
    for index in range(1, n_tensor):
        reward = reward + vote_ref[index]
    reward = reward / positions
    margin = reward[8:16] - reward[:8]
    margin_ref[...] = margin
    tiny = jnp.exp(-jnp.abs(margin))
    sigmoid_gap = jnp.where(margin >= 0.0, 1.0, tiny) / (1.0 + tiny)
    gain = sigmoid_gap[:1] * (loss_scale / positions)
    gain2 = jnp.concatenate([gain, gain], axis=1)

    def give(part):
        factor = gain2 if part else gain2 * scale
        for strip in strips:
            piece_ref[part, strip, :] = (gpf_ref[part, strip, :] * factor).astype(jnp.bfloat16)
        index = 0
        for kind, dz in ((3, 2), (1, 1), (2, -1), (0, 0)):
            for c in range(2) if kind else (1 - core,):
                target = me.at(dz if kind != 3 else 4 * c - 2, 0, c)
                push(
                    piece_ref.at[part, place(me.block(dz, c))],
                    got_ref.at[part, 2 * kind + core],
                    cb_send.at[part, index],
                    cb_recv.at[part, 2 * kind + core],
                    target,
                )
                index += 1
        got_ref[part, core] = piece_ref[part, place(me.block(0, core)), :]

    names = [
        name(me.at(dz, 0, c)) for kind, dz in ((0, 0), (1, -1), (2, 1), (3, far)) for c in range(2)
    ]
    chunk = 16
    lanes = 128
    turns = (2, 1, 3, 0)

    def add(left_ref, right_ref):
        return left_ref[...].astype(jnp.float32) + right_ref[...].astype(jnp.float32)

    def collect(part):
        for kind in range(4):
            for c in range(2) if kind else (1 - core,):
                landed(got_ref.at[part, 2 * kind + c], cb_recv.at[part, 2 * kind + c])
        for order, dzh in enumerate(turns):
            base = lax.rem(me.high + dzh, LONG) * WIDE
            for dx in turns:
                prompt = base + lax.rem(me.x + dx, WIDE)
                picks = [jnp.where(each == prompt, 1.0, 0.0) for each in names]

                def select(index, carry):
                    row = pl.ds(pl.multiple_of(index * chunk, chunk), chunk)
                    for start in range(0, wide, lanes):
                        column = slice(start, start + lanes)
                        total = picks[0] * got_ref[part, 0, row, column].astype(jnp.float32)
                        for source in range(1, len(names)):
                            total += picks[source] * got_ref[part, source, row, column].astype(
                                jnp.float32
                            )
                        dense_ref[part, dzh, dx, row, column] = total.astype(jnp.bfloat16)
                    return carry

                lax.fori_loop(0, block_rows // chunk, select, 0)
                if dx == 2:
                    for side, target in enumerate((right, left)):
                        push(
                            dense_ref.at[part, dzh, dx, parts[side]],
                            x1_ref.at[part, side, dzh],
                            xb_send.at[part, 4 * order + side],
                            xb_recv.at[part, 4 * order + side],
                            target,
                        )

    def x_turn(part, order):
        dzh = turns[order]
        for side, (dx, target) in enumerate(((1, right), (3, left))):
            arrival = x1_ref.at[part, side, dzh]
            landed(arrival, xb_recv.at[part, 4 * order + side])
            block = dense_ref.at[part, dzh, dx]
            section = block.at[parts[side]]
            section[...] = add(section, arrival).astype(jnp.bfloat16)
            index = 4 * order + 2 + side
            push(
                block,
                x2_ref.at[part, side, dzh],
                xb_send.at[part, index],
                xb_recv.at[part, index],
                target,
            )

    def x_end(part, order):
        dzh = turns[order]
        for side in range(2):
            landed(x2_ref.at[part, side, dzh], xb_recv.at[part, 4 * order + 2 + side])
        total = add(x2_ref.at[part, 0, dzh], x2_ref.at[part, 1, dzh])
        total += dense_ref[part, dzh, 0].astype(jnp.float32)
        sum_ref[part, dzh] = total.astype(jnp.bfloat16)

    def z_begin(part):
        for side, target in enumerate((up, down)):
            push(
                sum_ref.at[part, 2, parts[side]],
                z1_ref.at[part, side],
                zb_send.at[part, side],
                zb_recv.at[part, side],
                target,
            )

    def z_turn(part):
        for side, (dzh, target) in enumerate(((1, up), (3, down))):
            arrival = z1_ref.at[part, side]
            landed(arrival, zb_recv.at[part, side])
            block = sum_ref.at[part, dzh]
            section = block.at[parts[side]]
            section[...] = add(section, arrival).astype(jnp.bfloat16)
            push(
                block,
                z2_ref.at[part, side],
                zb_send.at[part, 2 + side],
                zb_recv.at[part, 2 + side],
                target,
            )

    def z_end(part):
        for side in range(2):
            landed(z2_ref.at[part, side], zb_recv.at[part, 2 + side])
        total = add(z2_ref.at[part, 0], z2_ref.at[part, 1])
        total += sum_ref[part, 0].astype(jnp.float32)
        owned_ref[part] = total.astype(jnp.bfloat16)

    give(1)
    lax.fori_loop(count // 2, count, back_step, 0)
    give(0)
    collect(1)
    for order in range(LONG):
        x_turn(1, order)
    x_end(1, 0)
    z_begin(1)
    collect(0)
    x_end(1, 1)
    x_end(1, 2)
    z_turn(1)
    x_end(1, 3)
    for order in range(LONG):
        x_turn(0, order)
    x_end(0, 0)
    z_begin(0)

    def write_step(index, carry):
        member, start, lane, sign = where_is(index)
        factor = gain * (2 * member - 1).astype(jnp.float32)
        part = pl.ds(start, TILE)
        gq_ref[member, part, :] = (gqf_ref[member, part, :] * factor).astype(jnp.bfloat16)
        return carry

    lax.fori_loop(0, count, write_step, 0)
    for member in range(members):
        factor = gain2 if member else -gain2
        gr_ref[member, 0] = (grf_ref[member, 0] * (factor * scale)).astype(jnp.bfloat16)
        gr_ref[member, 1] = (grf_ref[member, 1] * factor).astype(jnp.bfloat16)

    x_end(0, 1)
    x_end(0, 2)
    z_turn(0)
    x_end(0, 3)
    z_end(1)
    z_end(0)
    for copy in sent:
        copy.wait_send()


def pair_call(prompt_of, prompt_len, q, own, rkv, w, n_tensor):
    members, rows, hd = q.shape
    _, block_rows, wide = own.shape
    positions = rkv.shape[2]
    heads = w.shape[0]
    n_prompt, n_resp = 2 * LONG, LONG * WIDE
    span = n_prompt * block_rows
    period = heads * TILE // math.gcd(heads, TILE)
    count = members * rows // TILE
    half = block_rows // 2
    vmem = pl.BlockSpec(memory_space=pltpu.VMEM)
    smem = pl.BlockSpec(memory_space=pltpu.SMEM)
    dma = pltpu.SemaphoreType.DMA
    low, full = jnp.bfloat16, jnp.float32

    def ways():
        return [dma((2, 4)), dma((2, 4)), dma((2, 16)), dma((2, 16)), dma((2, 8)), dma((2, 8))]

    return pl.pallas_call(
        pair_kernel,
        out_shape=(
            jax.ShapeDtypeStruct((members, rows, hd), low),
            jax.ShapeDtypeStruct((members, 2, positions, wide), low),
            jax.ShapeDtypeStruct((2, block_rows, wide), low),
            jax.ShapeDtypeStruct((8, hd), full),
        ),
        in_specs=[smem] * 2 + [vmem] * 4,
        out_specs=(vmem,) * 4,
        scratch_shapes=[
            pltpu.VMEM((n_resp, block_rows, wide), low),
            pltpu.VMEM((n_resp, block_rows, wide), low),
            pltpu.VMEM((2, n_prompt - 1, block_rows, wide), low),
            pltpu.VMEM((2, span, wide), low),
            pltpu.VMEM((period, hd), full),
            pltpu.VMEM((hd, period), full),
            pltpu.VMEM((period, hd), low),
            pltpu.VMEM((hd, period), full),
            pltpu.VMEM((period, wide), low),
            pltpu.VMEM((wide, period), low),
            pltpu.VMEM((wide, span), low),
            pltpu.VMEM((wide, span), low),
            pltpu.VMEM((members, wide, positions), low),
            pltpu.VMEM((members, wide, positions), low),
            pltpu.VMEM((span, period), full),
            pltpu.VMEM((members, positions, period), full),
            pltpu.VMEM((count, span, TILE), full),
            pltpu.VMEM((count, positions, TILE), full),
            pltpu.VMEM((count, span, TILE), low),
            pltpu.VMEM((16, TILE), full),
            pltpu.VMEM((8, TILE), full),
            pltpu.VMEM((members, rows, hd), full),
            pltpu.VMEM((2, span, wide), full),
            pltpu.VMEM((members, 2, positions, wide), full),
            pltpu.VMEM((n_tensor, 8 * members, hd), full),
            pltpu.VMEM((2, span, wide), low),
            pltpu.VMEM((2, n_prompt, block_rows, wide), low),
            pltpu.VMEM((2, LONG, WIDE, block_rows, wide), low),
            pltpu.VMEM((2, LONG, block_rows, wide), low),
            pltpu.VMEM((2, 2, LONG, half, wide), low),
            pltpu.VMEM((2, 2, LONG, block_rows, wide), low),
            pltpu.VMEM((2, 2, half, wide), low),
            pltpu.VMEM((2, 2, block_rows, wide), low),
            *ways(),
            dma((n_tensor - 1,)),
            dma((n_tensor - 1,)),
            *ways(),
        ],
        compiler_params=pltpu.CompilerParams(
            collective_id=0, has_side_effects=True, vmem_limit_bytes=56 * 2**20
        ),
    )(prompt_of, prompt_len, q, own, rkv, w)


def pack(kv):
    flat = jnp.moveaxis(kv, -2, -4)
    return flat.reshape(flat.shape[:-2] + (-1,))


def unpack(flat, kv_heads):
    split = flat.reshape(flat.shape[:-1] + (kv_heads, -1))
    return jnp.moveaxis(split, -4, -2)


def shards(queries, resp_kv, prompt_kv, prompt_of, prompt_len, reward_head):
    _, members, positions, heads, hd = queries.shape
    kv_heads = prompt_kv.shape[2]
    q = queries.reshape(members, positions * heads, hd)
    gq, gr, owned, margin = pair_call(
        prompt_of,
        prompt_len,
        q,
        pack(prompt_kv[0]),
        pack(resp_kv[0]),
        reward_head,
        lax.axis_size("tensor"),
    )
    pair_loss = jnp.logaddexp(0.0, margin[0, :1])
    return (
        pair_loss,
        gq.reshape(queries.shape),
        unpack(gr, kv_heads)[None],
        unpack(owned, kv_heads)[None],
    )


def solution(mesh):
    in_specs = (
        P(("prompt", "resp"), None, None, "tensor", None),
        P(("prompt", "resp"), None, None, "tensor", None, None),
        P("resp", "prompt", "tensor", None, None),
        P(),
        P(),
        P("tensor", None),
    )
    out_specs = (
        P(("prompt", "resp")),
        P(("prompt", "resp"), None, None, "tensor", None),
        P(("prompt", "resp"), None, None, "tensor", None, None),
        P("resp", "prompt", "tensor", None, None),
    )
    return jax.shard_map(shards, mesh=mesh, in_specs=in_specs, out_specs=out_specs, check_vma=False)
```

```python
import math

import jax
import jax.numpy as jnp
from jax import lax
from jax.experimental import pallas as pl
from jax.experimental.pallas import tpu as pltpu
from jax.sharding import PartitionSpec as P

BLOCK = 128
TILE = 256

loss_scale = 8192.0


def product(left, right):
    return jnp.dot(left, right, preferred_element_type=jnp.float32)


def product_nt(left, right):
    return lax.dot_general(
        left, right, (((1,), (1,)), ((), ())), preferred_element_type=jnp.float32
    )


LONG = 4
WIDE = 4
MESH = pl.DeviceIdType.MESH


class Place:
    def __init__(self):
        prompt = lax.axis_index("prompt")
        resp = lax.axis_index("resp")
        self.core = lax.rem(prompt, 2)
        self.low = lax.div(prompt, 2)
        self.high = lax.div(resp, WIDE)
        self.x = lax.rem(resp, WIDE)
        self.tensor = lax.axis_index("tensor")
        self.z = self.high * LONG + self.low

    def at(self, dz, dx, core):
        ring = LONG * LONG
        z = lax.rem(self.z + dz + ring, ring)
        x = lax.rem(self.x + dx + WIDE, WIDE)
        return (lax.rem(z, LONG) * 2 + core, lax.div(z, LONG) * WIDE + x, self.tensor)

    def block(self, dz, core):
        return lax.rem(self.low + dz + LONG, LONG) * 2 + core


def remote(src, dst, send, recv, target):
    return pltpu.make_async_remote_copy(
        src_ref=src,
        dst_ref=dst,
        send_sem=send,
        recv_sem=recv,
        device_id=target,
        device_id_type=MESH,
    )


def pair_kernel(
    prompt_of_ref,
    prompt_len_ref,
    q_ref,
    own_ref,
    rkv_ref,
    w_ref,
    gq_ref,
    gr_ref,
    owned_ref,
    loss_ref,
    all_k_ref,
    all_v_ref,
    out_ref,
    whole_ref,
    wrow_ref,
    wt_ref,
    mask_ref,
    mask_t_ref,
    w2_ref,
    w2t_ref,
    rk_ref,
    rv_ref,
    kt_ref,
    vt_ref,
    rkt_ref,
    rvt_ref,
    dp_ref,
    drp_ref,
    low_ref,
    w2i_ref,
    q2i_ref,
    inverse_ref,
    delta_ref,
    reward_ref,
    gqf_ref,
    vote_ref,
    gain_ref,
    factor_ref,
    piece_ref,
    got_ref,
    dense_ref,
    sum_ref,
    grf_ref,
    x1_ref,
    x2_ref,
    z1_ref,
    z2_ref,
    z_send,
    z_recv,
    x_send,
    x_recv,
    c_send,
    c_recv,
    y_send,
    y_recv,
    g_send,
    g_recv,
    zb_send,
    zb_recv,
    xb_send,
    xb_recv,
    cb_send,
    cb_recv,
):
    members, rows, hd = q_ref.shape
    block_rows = own_ref.shape[0]
    span = whole_ref.shape[1]
    positions = rkv_ref.shape[1]
    heads = w_ref.shape[0]
    blocks = span // BLOCK
    period = wrow_ref.shape[0]
    phases = period // TILE
    tiles = rows // TILE
    wide = 2 * hd
    scale = hd**-0.5
    pace = scale * math.log2(math.e)
    n_resp = LONG * WIDE
    n_tensor = vote_ref.shape[0]
    count = members * tiles
    keys = pl.ds(0, span)
    tail = pl.ds(span, positions)

    def pick(flat, part):
        lows = [slice((2 * g + part) * hd, (2 * g + part + 1) * hd) for g in range(2)]
        return jnp.concatenate([flat[:, low] for low in lows], axis=1)

    def unpick(ref, part, value):
        for g in range(2):
            low = (2 * g + part) * hd
            ref[:, low : low + hd] = value[:, g * hd : (g + 1) * hd]

    me = Place()
    core = me.core
    half = block_rows // 2
    parts = (pl.ds(0, half), pl.ds(half, half))
    up, down = me.at(LONG, 0, core), me.at(-LONG, 0, core)
    right, left = me.at(0, 1, core), me.at(0, -1, core)
    far = 2 - 4 * core
    here = me.at(0, 0, core)
    peers = [
        (here[0], here[1], lax.rem(me.tensor + step, n_tensor)) for step in range(1, n_tensor)
    ]
    barrier = pltpu.get_barrier_semaphore()
    friends = (
        [up, down, right, left, me.at(0, 0, 1 - core)]
        + [me.at(dz, 0, c) for dz in (1, -1) for c in range(2)]
        + [me.at(-2, 0, 0), me.at(2, 0, 1), me.at(far, 0, core)]
        + peers
    )
    for device in friends:
        pl.semaphore_signal(barrier, inc=1, device_id=device, device_id_type=MESH)
    pl.semaphore_wait(barrier, len(friends))

    sent = []

    def push(src, dst, send, recv, target):
        copy = remote(src, dst, send, recv, target)
        copy.start()
        sent.append(copy)

    def landed(ref, recv):
        remote(ref, ref, y_send.at[0], recv, up).wait_recv()

    def slot(dzh, dx):
        return lax.rem(me.high + dzh + LONG, LONG) * WIDE + lax.rem(me.x + dx + WIDE, WIDE)

    tables = (all_k_ref, all_v_ref)

    def spread(part, order, dzh):
        block = tables[part].at[slot(dzh, 0)]
        for side, target in enumerate((right, left)):
            index = 4 * order + side
            push(block, block, x_send.at[part, index], x_recv.at[part, index], target)

    def relay(part, order, dzh):
        for side, (dx, target) in enumerate(((-1, right), (1, left))):
            block = tables[part].at[slot(dzh, dx)]
            landed(block, x_recv.at[part, 4 * order + side])
            section = block.at[parts[side]]
            index = 4 * order + 2 + side
            push(section, section, x_send.at[part, index], x_recv.at[part, index], target)

    def begin(part):
        tables[part][slot(0, 0)] = pick(own_ref[...], part)
        block = tables[part].at[slot(0, 0)]
        push(block, block, z_send.at[part, 0], z_recv.at[part, 0], up)
        push(block, block, z_send.at[part, 1], z_recv.at[part, 1], down)
        spread(part, 0, 0)

    def turn(part):
        for side, (dzh, target) in enumerate(((-1, up), (1, down))):
            block = tables[part].at[slot(dzh, 0)]
            landed(block, z_recv.at[part, side])
            section = block.at[parts[side]]
            push(section, section, z_send.at[part, 2 + side], z_recv.at[part, 2 + side], target)

    def middle(part):
        spread(part, 1, -1)
        spread(part, 2, 1)
        relay(part, 0, 0)

    def opposite(part):
        block = tables[part].at[slot(2, 0)]
        for side in range(2):
            landed(block.at[parts[side]], z_recv.at[part, 2 + side])
        spread(part, 3, 2)

    def relays(part):
        for order, dzh in ((1, -1), (2, 1), (3, 2)):
            relay(part, order, dzh)

    def complete(part):
        for order, dzh in ((0, 0), (1, -1), (2, 1), (3, 2)):
            block = tables[part].at[slot(dzh, 2)]
            for side in range(2):
                landed(block.at[parts[side]], x_recv.at[part, 4 * order + 2 + side])

    def place(device_block):
        return pl.ds(pl.multiple_of(device_block * block_rows, block_rows), block_rows)

    def name(device):
        return prompt_of_ref[device[0] * n_resp + device[1]]

    def deliver(part):
        mine = whole_ref.at[part, place(me.block(0, core))]
        index = 0
        for kind, dz in ((3, far), (1, 1), (2, -1), (0, 0)):
            for c in range(2) if kind else (1 - core,):
                target = me.at(dz, 0, c)
                out_ref[part, index] = tables[part][name(target)]
                push(
                    out_ref.at[part, index],
                    mine,
                    c_send.at[part, index],
                    c_recv.at[part, 2 * kind + core],
                    target,
                )
                index += 1
        mine[...] = tables[part][name(here)]

    def receive(part):
        for kind, dz in ((0, 0), (1, -1), (2, 1), (3, 2)):
            for c in range(2) if kind else (1 - core,):
                landed(whole_ref.at[part, place(me.block(dz, c))], c_recv.at[part, 2 * kind + c])

    begin(0)

    for index in range(period // heads):
        wrow_ref[index * heads : (index + 1) * heads, :] = w_ref[...]
    for phase in range(phases):
        part = slice(phase * TILE, (phase + 1) * TILE)
        row = lax.broadcasted_iota(jnp.int32, (TILE, hd), 0) + phase * TILE
        first = (lax.rem(row, heads) < heads // 2).astype(jnp.float32)
        wrow = wrow_ref[part, :]
        mask_ref[part, :] = first.astype(jnp.bfloat16)
        mask_t_ref[:, part] = first.T
        wt_ref[:, part] = wrow.T
        w2 = jnp.concatenate([wrow * first, wrow * (1.0 - first)], axis=1)
        w2_ref[part, :] = w2.astype(jnp.bfloat16)
        w2t_ref[:, part] = w2.T.astype(jnp.bfloat16)
    for member in range(members):
        rk_ref[member] = pick(rkv_ref[member], 0)
        rv_ref[member] = pick(rkv_ref[member], 1)
        rkt_ref[member] = rk_ref[member].astype(jnp.float32).T.astype(jnp.bfloat16)
        rvt_ref[member] = rv_ref[member].astype(jnp.float32).T.astype(jnp.bfloat16)
        drp_ref[member] = product(rv_ref[member], w2t_ref[...])
    reward_ref[...] = jnp.zeros_like(reward_ref)

    turn(0)
    begin(1)
    middle(0)
    opposite(0)
    relays(0)
    turn(1)
    complete(0)
    deliver(0)
    middle(1)
    opposite(1)
    relays(1)
    complete(1)
    deliver(1)

    length = prompt_len_ref[name(here)]
    shades = [jnp.where(block < length, 0.0, -1e30) for block in range(blocks)]
    strips = [slice(block * BLOCK, (block + 1) * BLOCK) for block in range(blocks)]

    PAIRED = 2

    def where_is(index):
        member = lax.div(index, tiles)
        start = pl.multiple_of(lax.rem(index, tiles) * TILE, TILE)
        lane = pl.ds(pl.multiple_of(lax.rem(index, phases) * TILE, TILE), TILE)
        column = pl.ds(pl.multiple_of(index * TILE, TILE), TILE)
        sign = (2 * member - 1).astype(jnp.float32)
        return member, start, lane, column, sign

    def paired(step):
        def body(index, carry):
            for sub in range(PAIRED):
                step(index * PAIRED + sub)
            return carry

        return body

    def run(step, first, last):
        lax.fori_loop(first // PAIRED, last // PAIRED, paired(step), 0)

    wider = 2 * BLOCK
    broad = [slice(start, start + wider) for start in range(0, span, wider)]

    def score_step(index):
        member, start, lane, column, sign = where_is(index)
        q = q_ref[member, pl.ds(start, TILE), :]
        first = mask_ref[lane, :]
        q2 = jnp.concatenate([q * first, q * (1 - first)], axis=1)
        sr = product_nt(rk_ref[member], q2)
        causal = (
            lax.broadcasted_iota(jnp.int32, (positions, TILE), 0) * heads
            <= lax.broadcasted_iota(jnp.int32, (positions, TILE), 1) + start
        )
        sr = jnp.where(causal, sr, -1e30)
        highest = jnp.max(sr, axis=0, keepdims=True)
        for number, part in enumerate(broad):
            s = product_nt(whole_ref[0, part, :], q2)
            for sub in range(2):
                top = jnp.max(s[sub * BLOCK : (sub + 1) * BLOCK], axis=0, keepdims=True)
                highest = jnp.maximum(highest, top + shades[2 * number + sub])
        er = jnp.exp2((sr - highest) * pace)
        total = jnp.sum(er, axis=0, keepdims=True)
        low_ref[tail, column] = er.astype(jnp.bfloat16)
        for number, part in enumerate(broad):
            s = product_nt(whole_ref[0, part, :], q2)
            for sub in range(2):
                shifted = s[sub * BLOCK : (sub + 1) * BLOCK] - (highest - shades[2 * number + sub])
                e = jnp.exp2(shifted * pace)
                total = total + jnp.sum(e, axis=0, keepdims=True)
                low_ref[strips[2 * number + sub], column] = e.astype(jnp.bfloat16)
        inverse = 1.0 / total
        inverse_ref[pl.ds(index, 1), :] = inverse
        turned = jnp.broadcast_to(inverse * sign, (hd, TILE)).T
        qi = q.astype(jnp.float32) * turned
        wi = wrow_ref[lane, :].astype(jnp.bfloat16).astype(jnp.float32) * turned
        firstf = first.astype(jnp.float32)
        q2i_ref[column, :] = jnp.concatenate([qi * firstf, qi * (1 - firstf)], axis=1).astype(
            jnp.bfloat16
        )
        w2i_ref[column, :] = jnp.concatenate([wi * firstf, wi * (1 - firstf)], axis=1).astype(
            jnp.bfloat16
        )

    def out_step(index):
        member, start, lane, column, sign = where_is(index)
        both = product(vt_ref[...], low_ref[keys, column])
        both += product(rvt_ref[member], low_ref[tail, column])
        out = jnp.where(mask_t_ref[:, lane] > 0.5, both[:hd], both[hd:])
        out = (out * inverse_ref[pl.ds(index, 1), :]).astype(jnp.bfloat16).astype(jnp.float32)
        wt = wt_ref[:, lane]
        reward_ref[pl.ds(member, 1), :] += jnp.sum(out * wt, axis=0, keepdims=True)
        delta_ref[pl.ds(index, 1), :] = jnp.sum(
            out * wt.astype(jnp.bfloat16).astype(jnp.float32), axis=0, keepdims=True
        )

    def back_step(index):
        member, start, lane, column, sign = where_is(index)
        delta = delta_ref[pl.ds(index, 1), :]
        for strip in strips:
            low_ref[strip, column] = low_ref[strip, column] * (dp_ref[strip, lane] - delta).astype(
                jnp.bfloat16
            )
        dsr = low_ref[tail, column] * (drp_ref[member, :, lane] - delta).astype(jnp.bfloat16)
        low_ref[tail, column] = dsr
        both = product(kt_ref[...], low_ref[keys, column]) + product(rkt_ref[member], dsr)
        gq = jnp.where(mask_t_ref[:, lane] > 0.5, both[:hd], both[hd:])
        gq = gq * (inverse_ref[pl.ds(index, 1), :] * (sign * scale))
        gqf_ref[member, pl.ds(start, TILE), :] = gq.T

    def sums(part, left):
        right_ref = (q2i_ref, w2i_ref)[part]
        factor = 1.0 if part else scale
        for strip in left:
            value = product(low_ref[strip, :], right_ref[...]) * factor
            piece_ref[part, strip, :] = value.astype(jnp.bfloat16)

    def resp_sums(part):
        right_ref = (q2i_ref, w2i_ref)[part]
        factor = 1.0 if part else scale
        for member in range(members):
            column = slice(member * rows, (member + 1) * rows)
            grf_ref[member, part] = product(low_ref[tail, column], right_ref[column, :]) * factor

    def give(part):
        index = 0
        for kind, dz in ((3, 2), (1, 1), (2, -1), (0, 0)):
            for c in range(2) if kind else (1 - core,):
                push(
                    piece_ref.at[part, place(me.block(dz, c))],
                    got_ref.at[part, 2 * kind + core],
                    cb_send.at[part, index],
                    cb_recv.at[part, 2 * kind + core],
                    me.at(dz if kind != 3 else 4 * c - 2, 0, c),
                )
                index += 1
        got_ref[part, core] = piece_ref[part, place(me.block(0, core)), :]

    halves = [slice(0, span // 2), slice(span // 2, span)]
    receive(0)
    for strip in strips:
        kt_ref[:, strip] = whole_ref[0, strip, :].astype(jnp.float32).T.astype(jnp.bfloat16)
    run(score_step, 0, count)
    sums(1, halves)
    receive(1)
    give(1)
    for strip in strips:
        vt_ref[:, strip] = whole_ref[1, strip, :].astype(jnp.float32).T.astype(jnp.bfloat16)
    run(out_step, 0, count)

    ballot = vote_ref.at[me.tensor]
    for member in range(members):
        total = jnp.sum(reward_ref[member : member + 1, :], axis=1, keepdims=True)
        ballot[8 * member : 8 * (member + 1), :] = jnp.broadcast_to(total, (8, hd))
    for step, target in enumerate(peers):
        push(ballot, ballot, y_send.at[step], y_recv.at[step], target)
    resp_sums(1)
    dp_ref[...] = product(whole_ref[1], w2t_ref[...])
    run(back_step, 0, 4)

    for step in range(1, n_tensor):
        source = lax.rem(me.tensor + n_tensor - step, n_tensor)
        landed(vote_ref.at[source], y_recv.at[step - 1])
    reward = vote_ref[0]
    for index in range(1, n_tensor):
        reward = reward + vote_ref[index]
    reward = reward / positions
    margin = reward[8:16] - reward[:8]
    tiny = jnp.exp(-jnp.abs(margin))
    loss = jnp.maximum(margin, 0.0) + jnp.log1p(tiny)
    loss_ref[0] = loss[0, 0]
    sigmoid_gap = jnp.where(margin >= 0.0, 1.0, tiny) / (1.0 + tiny)
    gain = sigmoid_gap * (loss_scale / positions)
    gain_ref[core] = gain
    index = 0
    for kind, dz in ((3, 2), (1, 1), (2, -1), (0, 0)):
        for c in range(2) if kind else (1 - core,):
            push(
                gain_ref.at[core],
                gain_ref.at[2 * kind + core],
                g_send.at[index],
                g_recv.at[2 * kind + core],
                me.at(dz if kind != 3 else 4 * c - 2, 0, c),
            )
            index += 1

    names = [
        name(me.at(dz, 0, c)) for kind, dz in ((0, 0), (1, -1), (2, 1), (3, far)) for c in range(2)
    ]
    chunk = 16
    lanes = 128
    turns = (2, 1, 3, 0)
    sources = len(names)

    def factors():
        for kind in range(4):
            for c in range(2) if kind else (1 - core,):
                landed(gain_ref.at[2 * kind + c], g_recv.at[2 * kind + c])
        for a in range(LONG):
            for b in range(WIDE):
                prompt = slot(a, b)
                for source in range(sources):
                    row = (a * WIDE + b) * sources + source
                    share = jnp.where(names[source] == prompt, 1.0, 0.0)
                    factor_ref[row : row + 1, :] = gain_ref[source, :1, :] * share

    def add(left_ref, right_ref):
        return left_ref[...].astype(jnp.float32) + right_ref[...].astype(jnp.float32)

    def collect(part):
        for kind in range(4):
            for c in range(2) if kind else (1 - core,):
                landed(got_ref.at[part, 2 * kind + c], cb_recv.at[part, 2 * kind + c])

        def select(index, carry):
            row = pl.ds(pl.multiple_of(index * chunk, chunk), chunk)
            for start in range(0, wide, lanes):
                column = slice(start, start + lanes)
                terms = [
                    got_ref[part, source, row, column].astype(jnp.float32)
                    for source in range(sources)
                ]
                for a in range(LONG):
                    for b in range(WIDE):
                        base = (a * WIDE + b) * sources
                        total = terms[0] * factor_ref[base : base + 1, :]
                        for source in range(1, sources):
                            at = base + source
                            total += terms[source] * factor_ref[at : at + 1, :]
                        dense_ref[part, a, b, row, column] = total.astype(jnp.bfloat16)
            return carry

        lax.fori_loop(0, block_rows // chunk, select, 0)
        for order, dzh in enumerate(turns):
            for side, target in enumerate((right, left)):
                push(
                    dense_ref.at[part, dzh, 2, parts[side]],
                    x1_ref.at[part, side, dzh],
                    xb_send.at[part, 4 * order + side],
                    xb_recv.at[part, 4 * order + side],
                    target,
                )

    def x_turn(part, order):
        dzh = turns[order]
        for side, (dx, target) in enumerate(((1, right), (3, left))):
            arrival = x1_ref.at[part, side, dzh]
            landed(arrival, xb_recv.at[part, 4 * order + side])
            block = dense_ref.at[part, dzh, dx]
            section = block.at[parts[side]]
            section[...] = add(section, arrival).astype(jnp.bfloat16)
            index = 4 * order + 2 + side
            push(
                block,
                x2_ref.at[part, side, dzh],
                xb_send.at[part, index],
                xb_recv.at[part, index],
                target,
            )

    def x_end(part, order):
        dzh = turns[order]
        for side in range(2):
            landed(x2_ref.at[part, side, dzh], xb_recv.at[part, 4 * order + 2 + side])
        total = add(x2_ref.at[part, 0, dzh], x2_ref.at[part, 1, dzh])
        total += dense_ref[part, dzh, 0].astype(jnp.float32)
        sum_ref[part, dzh] = total.astype(jnp.bfloat16)

    def z_begin(part):
        for side, target in enumerate((up, down)):
            push(
                sum_ref.at[part, 2, parts[side]],
                z1_ref.at[part, side],
                zb_send.at[part, side],
                zb_recv.at[part, side],
                target,
            )

    def z_turn(part):
        for side, (dzh, target) in enumerate(((1, up), (3, down))):
            arrival = z1_ref.at[part, side]
            landed(arrival, zb_recv.at[part, side])
            block = sum_ref.at[part, dzh]
            section = block.at[parts[side]]
            section[...] = add(section, arrival).astype(jnp.bfloat16)
            push(
                block,
                z2_ref.at[part, side],
                zb_send.at[part, 2 + side],
                zb_recv.at[part, 2 + side],
                target,
            )

    def z_end(part):
        for side in range(2):
            landed(z2_ref.at[part, side], zb_recv.at[part, 2 + side])
        total = add(z2_ref.at[part, 0], z2_ref.at[part, 1])
        total += sum_ref[part, 0].astype(jnp.float32)
        unpick(owned_ref, part, total.astype(jnp.bfloat16))

    run(back_step, 4, 8)
    factors()
    collect(1)
    run(back_step, 8, 10)
    for order in range(LONG):
        x_turn(1, order)
    run(back_step, 10, 12)
    sums(0, halves)
    give(0)
    x_end(1, 0)
    z_begin(1)
    x_end(1, 1)
    x_end(1, 2)
    z_turn(1)
    x_end(1, 3)
    resp_sums(0)

    def write_step(index):
        member, start, lane, column, sign = where_is(index)
        part = pl.ds(start, TILE)
        gq_ref[member, part, :] = (gqf_ref[member, part, :] * gain_ref[core, :1, :]).astype(
            jnp.bfloat16
        )

    run(write_step, 0, count)
    gain2 = jnp.concatenate([gain[:1], gain[:1]], axis=1)
    for member in range(members):
        for part in range(2):
            unpick(gr_ref.at[member], part, (grf_ref[member, part] * gain2).astype(jnp.bfloat16))
    collect(0)
    z_end(1)
    for order in range(LONG):
        x_turn(0, order)
    x_end(0, 0)
    z_begin(0)
    x_end(0, 1)
    x_end(0, 2)
    z_turn(0)
    x_end(0, 3)
    z_end(0)
    for copy in sent:
        copy.wait_send()


def pair_call(prompt_of, prompt_len, q, own, rkv, w, n_tensor):
    members, rows, hd = q.shape
    block_rows = own.shape[0]
    wide = own.shape[1] // 2
    positions = rkv.shape[1]
    heads = w.shape[0]
    n_prompt, n_resp = 2 * LONG, LONG * WIDE
    span = n_prompt * block_rows
    period = heads * TILE // math.gcd(heads, TILE)
    count = members * rows // TILE
    half = block_rows // 2
    vmem = pl.BlockSpec(memory_space=pltpu.VMEM)
    smem = pl.BlockSpec(memory_space=pltpu.SMEM)
    dma = pltpu.SemaphoreType.DMA
    low, full = jnp.bfloat16, jnp.float32

    def ways():
        return [dma((2, 4)), dma((2, 4)), dma((2, 16)), dma((2, 16)), dma((2, 8)), dma((2, 8))]

    return pl.pallas_call(
        pair_kernel,
        out_shape=(
            jax.ShapeDtypeStruct((members, rows, hd), low),
            jax.ShapeDtypeStruct((members, positions, 2 * wide), low),
            jax.ShapeDtypeStruct((block_rows, 2 * wide), low),
            jax.ShapeDtypeStruct((1,), full),
        ),
        in_specs=[smem] * 2 + [vmem] * 4,
        out_specs=(vmem, vmem, vmem, smem),
        scratch_shapes=[
            pltpu.VMEM((n_resp, block_rows, wide), low),
            pltpu.VMEM((n_resp, block_rows, wide), low),
            pltpu.VMEM((2, n_prompt - 1, block_rows, wide), low),
            pltpu.VMEM((2, span, wide), low),
            pltpu.VMEM((period, hd), full),
            pltpu.VMEM((hd, period), full),
            pltpu.VMEM((period, hd), low),
            pltpu.VMEM((hd, period), full),
            pltpu.VMEM((period, wide), low),
            pltpu.VMEM((wide, period), low),
            pltpu.VMEM((members, positions, wide), low),
            pltpu.VMEM((members, positions, wide), low),
            pltpu.VMEM((wide, span), low),
            pltpu.VMEM((wide, span), low),
            pltpu.VMEM((members, wide, positions), low),
            pltpu.VMEM((members, wide, positions), low),
            pltpu.VMEM((span, period), full),
            pltpu.VMEM((members, positions, period), full),
            pltpu.VMEM((span + positions, count * TILE), low),
            pltpu.VMEM((count * TILE, wide), low),
            pltpu.VMEM((count * TILE, wide), low),
            pltpu.VMEM((16, TILE), full),
            pltpu.VMEM((16, TILE), full),
            pltpu.VMEM((8, TILE), full),
            pltpu.VMEM((members, rows, hd), full),
            pltpu.VMEM((n_tensor, 8 * members, hd), full),
            pltpu.VMEM((n_prompt, 8, hd), full),
            pltpu.VMEM((n_prompt * n_resp, hd), full),
            pltpu.VMEM((2, span, wide), low),
            pltpu.VMEM((2, n_prompt, block_rows, wide), low),
            pltpu.VMEM((2, LONG, WIDE, block_rows, wide), low),
            pltpu.VMEM((2, LONG, block_rows, wide), low),
            pltpu.VMEM((members, 2, positions, wide), full),
            pltpu.VMEM((2, 2, LONG, half, wide), low),
            pltpu.VMEM((2, 2, LONG, block_rows, wide), low),
            pltpu.VMEM((2, 2, half, wide), low),
            pltpu.VMEM((2, 2, block_rows, wide), low),
            *ways(),
            dma((n_tensor - 1,)),
            dma((n_tensor - 1,)),
            dma((n_prompt,)),
            dma((n_prompt,)),
            *ways(),
        ],
        compiler_params=pltpu.CompilerParams(
            collective_id=0, has_side_effects=True, vmem_limit_bytes=56 * 2**20
        ),
    )(prompt_of, prompt_len, q, own, rkv, w)


def shards(queries, resp_kv, prompt_kv, prompt_of, prompt_len, reward_head):
    _, members, positions, heads, hd = queries.shape
    gq, gr, owned, pair_loss = pair_call(
        prompt_of,
        prompt_len,
        queries.reshape(members, positions * heads, hd),
        prompt_kv.reshape(prompt_kv.shape[1], -1),
        resp_kv.reshape(members, positions, -1),
        reward_head,
        lax.axis_size("tensor"),
    )
    return (
        pair_loss,
        gq.reshape(queries.shape),
        gr.reshape(resp_kv.shape),
        owned.reshape(prompt_kv.shape),
    )


def solution(mesh):
    in_specs = (
        P(("prompt", "resp"), None, None, "tensor", None),
        P(("prompt", "resp"), None, None, "tensor", None, None),
        P("resp", "prompt", "tensor", None, None),
        P(),
        P(),
        P("tensor", None),
    )
    out_specs = (
        P(("prompt", "resp")),
        P(("prompt", "resp"), None, None, "tensor", None),
        P(("prompt", "resp"), None, None, "tensor", None, None),
        P("resp", "prompt", "tensor", None, None),
    )
    return jax.shard_map(shards, mesh=mesh, in_specs=in_specs, out_specs=out_specs, check_vma=False)
```

```python
import math

import jax
import jax.numpy as jnp
from jax import lax
from jax.experimental import pallas as pl
from jax.experimental.pallas import tpu as pltpu
from jax.sharding import PartitionSpec as P

BLOCK = 128
TILE = 256

loss_scale = 8192.0


def product(left, right):
    return jnp.dot(left, right, preferred_element_type=jnp.float32)


def product_nt(left, right):
    return lax.dot_general(
        left, right, (((1,), (1,)), ((), ())), preferred_element_type=jnp.float32
    )


LONG = 4
WIDE = 4
MESH = pl.DeviceIdType.MESH


class Place:
    def __init__(self):
        prompt = lax.axis_index("prompt")
        resp = lax.axis_index("resp")
        self.core = lax.rem(prompt, 2)
        self.low = lax.div(prompt, 2)
        self.high = lax.div(resp, WIDE)
        self.x = lax.rem(resp, WIDE)
        self.tensor = lax.axis_index("tensor")
        self.z = self.high * LONG + self.low

    def at(self, dz, dx, core):
        ring = LONG * LONG
        z = lax.rem(self.z + dz + ring, ring)
        x = lax.rem(self.x + dx + WIDE, WIDE)
        return (lax.rem(z, LONG) * 2 + core, lax.div(z, LONG) * WIDE + x, self.tensor)

    def block(self, dz, core):
        return lax.rem(self.low + dz + LONG, LONG) * 2 + core


def remote(src, dst, send, recv, target):
    return pltpu.make_async_remote_copy(
        src_ref=src,
        dst_ref=dst,
        send_sem=send,
        recv_sem=recv,
        device_id=target,
        device_id_type=MESH,
    )


def pair_kernel(
    prompt_of_ref,
    prompt_len_ref,
    q_hbm_ref,
    own_ref,
    rkv_ref,
    w_ref,
    gq_hbm_ref,
    gr_ref,
    owned_ref,
    loss_ref,
    all_k_ref,
    all_v_ref,
    out_ref,
    whole_ref,
    q_ref,
    gq_ref,
    wrow_ref,
    wt_ref,
    mask_ref,
    mask_t_ref,
    w2_ref,
    w2t_ref,
    rk_ref,
    rv_ref,
    kt_ref,
    vt_ref,
    rkt_ref,
    rvt_ref,
    dp_ref,
    drp_ref,
    low_ref,
    w2i_ref,
    q2i_ref,
    inverse_ref,
    delta_ref,
    reward_ref,
    gqf_ref,
    vote_ref,
    gain_ref,
    factor_ref,
    piece_ref,
    got_ref,
    dense_ref,
    sum_ref,
    grf_ref,
    x2_ref,
    z1_ref,
    z2_ref,
    z_send,
    z_recv,
    x_send,
    x_recv,
    c_send,
    c_recv,
    y_send,
    y_recv,
    g_send,
    g_recv,
    zb_send,
    zb_recv,
    xb_send,
    xb_recv,
    cb_send,
    cb_recv,
    io_sem,
):
    members, rows, hd = q_ref.shape
    block_rows = own_ref.shape[0]
    span = whole_ref.shape[1]
    positions = rkv_ref.shape[1]
    heads = w_ref.shape[0]
    blocks = span // BLOCK
    period = wrow_ref.shape[0]
    phases = period // TILE
    tiles = rows // TILE
    wide = 2 * hd
    scale = hd**-0.5
    pace = scale * math.log2(math.e)
    n_resp = LONG * WIDE
    n_tensor = vote_ref.shape[0]
    count = members * tiles
    keys = pl.ds(0, span)
    tail = pl.ds(span, positions)

    def pick(flat, part):
        lows = [slice((2 * g + part) * hd, (2 * g + part + 1) * hd) for g in range(2)]
        return jnp.concatenate([flat[:, low] for low in lows], axis=1)

    def unpick(ref, part, value):
        for g in range(2):
            low = (2 * g + part) * hd
            ref[:, low : low + hd] = value[:, g * hd : (g + 1) * hd]

    q_copy = pltpu.make_async_copy(q_hbm_ref, q_ref, io_sem.at[0])
    q_copy.start()
    me = Place()
    core = me.core
    half = block_rows // 2
    parts = (pl.ds(0, half), pl.ds(half, half))
    up, down = me.at(LONG, 0, core), me.at(-LONG, 0, core)
    right, left = me.at(0, 1, core), me.at(0, -1, core)
    across = me.at(0, 2, core)
    sides = (right, left, across)
    far = 2 - 4 * core
    here = me.at(0, 0, core)
    peers = [
        (here[0], here[1], lax.rem(me.tensor + step, n_tensor)) for step in range(1, n_tensor)
    ]
    barrier = pltpu.get_barrier_semaphore()
    friends = (
        [up, down, right, left, me.at(0, 0, 1 - core)]
        + [me.at(dz, 0, c) for dz in (1, -1) for c in range(2)]
        + [me.at(-2, 0, 0), me.at(2, 0, 1), me.at(far, 0, core)]
        + [across]
        + peers
    )
    for device in friends:
        pl.semaphore_signal(barrier, inc=1, device_id=device, device_id_type=MESH)
    pl.semaphore_wait(barrier, len(friends))

    sent = []

    def push(src, dst, send, recv, target):
        copy = remote(src, dst, send, recv, target)
        copy.start()
        sent.append(copy)

    def landed(ref, recv):
        remote(ref, ref, y_send.at[0], recv, up).wait_recv()

    def slot(dzh, dx):
        return lax.rem(me.high + dzh + LONG, LONG) * WIDE + lax.rem(me.x + dx + WIDE, WIDE)

    tables = (all_k_ref, all_v_ref)

    def spread(part, order, dzh):
        block = tables[part].at[slot(dzh, 0)]
        for side, target in enumerate(sides):
            index = 4 * order + side
            push(block, block, x_send.at[part, index], x_recv.at[part, index], target)

    def begin(part):
        tables[part][slot(0, 0)] = pick(own_ref[...], part)
        block = tables[part].at[slot(0, 0)]
        push(block, block, z_send.at[part, 0], z_recv.at[part, 0], up)
        push(block, block, z_send.at[part, 1], z_recv.at[part, 1], down)
        spread(part, 0, 0)

    def turn(part):
        for side, (dzh, target) in enumerate(((-1, up), (1, down))):
            block = tables[part].at[slot(dzh, 0)]
            landed(block, z_recv.at[part, side])
            section = block.at[parts[side]]
            push(section, section, z_send.at[part, 2 + side], z_recv.at[part, 2 + side], target)

    def middle(part):
        spread(part, 1, -1)
        spread(part, 2, 1)

    def opposite(part):
        block = tables[part].at[slot(2, 0)]
        for side in range(2):
            landed(block.at[parts[side]], z_recv.at[part, 2 + side])
        spread(part, 3, 2)

    def complete(part):
        for order, dzh in enumerate((0, -1, 1, 2)):
            for side, dx in enumerate((-1, 1, 2)):
                landed(tables[part].at[slot(dzh, dx)], x_recv.at[part, 4 * order + side])

    def place(device_block):
        return pl.ds(pl.multiple_of(device_block * block_rows, block_rows), block_rows)

    def name(device):
        return prompt_of_ref[device[0] * n_resp + device[1]]

    def deliver(part):
        mine = whole_ref.at[part, place(me.block(0, core))]
        index = 0
        for kind, dz in ((3, far), (1, 1), (2, -1), (0, 0)):
            for c in range(2) if kind else (1 - core,):
                target = me.at(dz, 0, c)
                out_ref[part, index] = tables[part][name(target)]
                push(
                    out_ref.at[part, index],
                    mine,
                    c_send.at[part, index],
                    c_recv.at[part, 2 * kind + core],
                    target,
                )
                index += 1
        mine[...] = tables[part][name(here)]

    def receive(part):
        for kind, dz in ((0, 0), (1, -1), (2, 1), (3, 2)):
            for c in range(2) if kind else (1 - core,):
                landed(whole_ref.at[part, place(me.block(dz, c))], c_recv.at[part, 2 * kind + c])

    begin(0)

    for index in range(period // heads):
        wrow_ref[index * heads : (index + 1) * heads, :] = w_ref[...]
    for phase in range(phases):
        part = slice(phase * TILE, (phase + 1) * TILE)
        row = lax.broadcasted_iota(jnp.int32, (TILE, hd), 0) + phase * TILE
        first = (lax.rem(row, heads) < heads // 2).astype(jnp.float32)
        wrow = wrow_ref[part, :]
        mask_ref[part, :] = first.astype(jnp.bfloat16)
        mask_t_ref[:, part] = first.T
        wt_ref[:, part] = wrow.T
        w2 = jnp.concatenate([wrow * first, wrow * (1.0 - first)], axis=1)
        w2_ref[part, :] = w2.astype(jnp.bfloat16)
        w2t_ref[:, part] = w2.T.astype(jnp.bfloat16)
    for member in range(members):
        rk_ref[member] = pick(rkv_ref[member], 0)
        rv_ref[member] = pick(rkv_ref[member], 1)
        rkt_ref[member] = rk_ref[member].astype(jnp.float32).T.astype(jnp.bfloat16)
        rvt_ref[member] = rv_ref[member].astype(jnp.float32).T.astype(jnp.bfloat16)
        drp_ref[member] = product(rv_ref[member], w2t_ref[...])
    reward_ref[...] = jnp.zeros_like(reward_ref)

    turn(0)
    begin(1)
    middle(0)
    opposite(0)
    turn(1)
    middle(1)
    complete(0)
    deliver(0)
    opposite(1)
    complete(1)
    deliver(1)

    length = prompt_len_ref[name(here)]
    shades = [jnp.where(block < length, 0.0, -1e30) for block in range(blocks)]
    strips = [slice(block * BLOCK, (block + 1) * BLOCK) for block in range(blocks)]

    PAIRED = 2

    def where_is(index):
        member = lax.div(index, tiles)
        start = pl.multiple_of(lax.rem(index, tiles) * TILE, TILE)
        lane = pl.ds(pl.multiple_of(lax.rem(index, phases) * TILE, TILE), TILE)
        column = pl.ds(pl.multiple_of(index * TILE, TILE), TILE)
        sign = (2 * member - 1).astype(jnp.float32)
        return member, start, lane, column, sign

    def paired(step):
        def body(index, carry):
            for sub in range(PAIRED):
                step(index * PAIRED + sub)
            return carry

        return body

    def run(step, first, last):
        lax.fori_loop(first // PAIRED, last // PAIRED, paired(step), 0)

    wider = 2 * BLOCK
    broad = [slice(start, start + wider) for start in range(0, span, wider)]

    def score_step(index):
        member, start, lane, column, sign = where_is(index)
        q = q_ref[member, pl.ds(start, TILE), :]
        first = mask_ref[lane, :]
        q2 = jnp.concatenate([q * first, q * (1 - first)], axis=1)
        sr = product_nt(rk_ref[member], q2)
        causal = (
            lax.broadcasted_iota(jnp.int32, (positions, TILE), 0) * heads
            <= lax.broadcasted_iota(jnp.int32, (positions, TILE), 1) + start
        )
        sr = jnp.where(causal, sr, -1e30)
        highest = jnp.max(sr, axis=0, keepdims=True)
        for number, part in enumerate(broad):
            s = product_nt(whole_ref[0, part, :], q2)
            for sub in range(2):
                top = jnp.max(s[sub * BLOCK : (sub + 1) * BLOCK], axis=0, keepdims=True)
                highest = jnp.maximum(highest, top + shades[2 * number + sub])
        er = jnp.exp2((sr - highest) * pace)
        total = jnp.sum(er, axis=0, keepdims=True)
        low_ref[tail, column] = er.astype(jnp.bfloat16)
        for number, part in enumerate(broad):
            s = product_nt(whole_ref[0, part, :], q2)
            for sub in range(2):
                shifted = s[sub * BLOCK : (sub + 1) * BLOCK] - (highest - shades[2 * number + sub])
                e = jnp.exp2(shifted * pace)
                total = total + jnp.sum(e, axis=0, keepdims=True)
                low_ref[strips[2 * number + sub], column] = e.astype(jnp.bfloat16)
        inverse = 1.0 / total
        inverse_ref[pl.ds(index, 1), :] = inverse
        turned = jnp.broadcast_to(inverse * sign, (hd, TILE)).T
        qi = q.astype(jnp.float32) * turned
        wi = wrow_ref[lane, :].astype(jnp.bfloat16).astype(jnp.float32) * turned
        firstf = first.astype(jnp.float32)
        q2i_ref[column, :] = jnp.concatenate([qi * firstf, qi * (1 - firstf)], axis=1).astype(
            jnp.bfloat16
        )
        w2i_ref[column, :] = jnp.concatenate([wi * firstf, wi * (1 - firstf)], axis=1).astype(
            jnp.bfloat16
        )

    def out_step(index):
        member, start, lane, column, sign = where_is(index)
        both = product(vt_ref[...], low_ref[keys, column])
        both += product(rvt_ref[member], low_ref[tail, column])
        out = jnp.where(mask_t_ref[:, lane] > 0.5, both[:hd], both[hd:])
        out = (out * inverse_ref[pl.ds(index, 1), :]).astype(jnp.bfloat16).astype(jnp.float32)
        wt = wt_ref[:, lane]
        reward_ref[pl.ds(member, 1), :] += jnp.sum(out * wt, axis=0, keepdims=True)
        delta_ref[pl.ds(index, 1), :] = jnp.sum(
            out * wt.astype(jnp.bfloat16).astype(jnp.float32), axis=0, keepdims=True
        )

    def back_step(index):
        member, start, lane, column, sign = where_is(index)
        delta = delta_ref[pl.ds(index, 1), :]
        for strip in strips:
            low_ref[strip, column] = low_ref[strip, column] * (dp_ref[strip, lane] - delta).astype(
                jnp.bfloat16
            )
        dsr = low_ref[tail, column] * (drp_ref[member, :, lane] - delta).astype(jnp.bfloat16)
        low_ref[tail, column] = dsr
        both = product(kt_ref[...], low_ref[keys, column]) + product(rkt_ref[member], dsr)
        gq = jnp.where(mask_t_ref[:, lane] > 0.5, both[:hd], both[hd:])
        gq = gq * (inverse_ref[pl.ds(index, 1), :] * (sign * scale))
        gqf_ref[member, pl.ds(start, TILE), :] = gq.T

    def sums(part, left):
        right_ref = (q2i_ref, w2i_ref)[part]
        factor = 1.0 if part else scale
        for strip in left:
            value = product(low_ref[strip, :], right_ref[...]) * factor
            piece_ref[part, strip, :] = value.astype(jnp.bfloat16)

    def resp_sums(part):
        right_ref = (q2i_ref, w2i_ref)[part]
        factor = 1.0 if part else scale
        for member in range(members):
            column = slice(member * rows, (member + 1) * rows)
            grf_ref[member, part] = product(low_ref[tail, column], right_ref[column, :]) * factor

    def give(part):
        index = 0
        for kind, dz in ((3, 2), (1, 1), (2, -1), (0, 0)):
            for c in range(2) if kind else (1 - core,):
                push(
                    piece_ref.at[part, place(me.block(dz, c))],
                    got_ref.at[part, 2 * kind + core],
                    cb_send.at[part, index],
                    cb_recv.at[part, 2 * kind + core],
                    me.at(dz if kind != 3 else 4 * c - 2, 0, c),
                )
                index += 1
        got_ref[part, core] = piece_ref[part, place(me.block(0, core)), :]

    halves = [slice(0, span // 2), slice(span // 2, span)]
    receive(0)
    for strip in strips:
        kt_ref[:, strip] = whole_ref[0, strip, :].astype(jnp.float32).T.astype(jnp.bfloat16)
    q_copy.wait()
    run(score_step, 0, count)
    sums(1, halves)
    receive(1)
    give(1)
    for strip in strips:
        vt_ref[:, strip] = whole_ref[1, strip, :].astype(jnp.float32).T.astype(jnp.bfloat16)
    run(out_step, 0, count)

    ballot = vote_ref.at[me.tensor]
    for member in range(members):
        total = jnp.sum(reward_ref[member : member + 1, :], axis=1, keepdims=True)
        ballot[8 * member : 8 * (member + 1), :] = jnp.broadcast_to(total, (8, hd))
    for step, target in enumerate(peers):
        push(ballot, ballot, y_send.at[step], y_recv.at[step], target)
    resp_sums(1)
    dp_ref[...] = product(whole_ref[1], w2t_ref[...])
    run(back_step, 0, 6)

    for step in range(1, n_tensor):
        source = lax.rem(me.tensor + n_tensor - step, n_tensor)
        landed(vote_ref.at[source], y_recv.at[step - 1])
    reward = vote_ref[0]
    for index in range(1, n_tensor):
        reward = reward + vote_ref[index]
    reward = reward / positions
    margin = reward[8:16] - reward[:8]
    tiny = jnp.exp(-jnp.abs(margin))
    loss = jnp.maximum(margin, 0.0) + jnp.log1p(tiny)
    loss_ref[0] = loss[0, 0]
    sigmoid_gap = jnp.where(margin >= 0.0, 1.0, tiny) / (1.0 + tiny)
    gain = sigmoid_gap * (loss_scale / positions)
    gain_ref[core] = gain
    index = 0
    for kind, dz in ((3, 2), (1, 1), (2, -1), (0, 0)):
        for c in range(2) if kind else (1 - core,):
            push(
                gain_ref.at[core],
                gain_ref.at[2 * kind + core],
                g_send.at[index],
                g_recv.at[2 * kind + core],
                me.at(dz if kind != 3 else 4 * c - 2, 0, c),
            )
            index += 1

    names = [
        name(me.at(dz, 0, c)) for kind, dz in ((0, 0), (1, -1), (2, 1), (3, far)) for c in range(2)
    ]
    chunk = 16
    lanes = 128
    turns = (2, 1, 3, 0)
    sources = len(names)

    def factors():
        for kind in range(4):
            for c in range(2) if kind else (1 - core,):
                landed(gain_ref.at[2 * kind + c], g_recv.at[2 * kind + c])
        for a in range(LONG):
            for b in range(WIDE):
                prompt = slot(a, b)
                for source in range(sources):
                    row = (a * WIDE + b) * sources + source
                    share = jnp.where(names[source] == prompt, 1.0, 0.0)
                    factor_ref[row : row + 1, :] = gain_ref[source, :1, :] * share

    def add(left_ref, right_ref):
        return left_ref[...].astype(jnp.float32) + right_ref[...].astype(jnp.float32)

    def collect(part):
        for kind in range(4):
            for c in range(2) if kind else (1 - core,):
                landed(got_ref.at[part, 2 * kind + c], cb_recv.at[part, 2 * kind + c])

        def select(index, carry):
            row = pl.ds(pl.multiple_of(index * chunk, chunk), chunk)
            for start in range(0, wide, lanes):
                column = slice(start, start + lanes)
                terms = [
                    got_ref[part, source, row, column].astype(jnp.float32)
                    for source in range(sources)
                ]
                for a in range(LONG):
                    for b in range(WIDE):
                        base = (a * WIDE + b) * sources
                        total = terms[0] * factor_ref[base : base + 1, :]
                        for source in range(1, sources):
                            at = base + source
                            total += terms[source] * factor_ref[at : at + 1, :]
                        dense_ref[part, a, b, row, column] = total.astype(jnp.bfloat16)
            return carry

        lax.fori_loop(0, block_rows // chunk, select, 0)
        for order, dzh in enumerate(turns):
            for side, (dx, target) in enumerate(zip((1, 3, 2), sides)):
                push(
                    dense_ref.at[part, dzh, dx],
                    x2_ref.at[part, side, dzh],
                    xb_send.at[part, 4 * order + side],
                    xb_recv.at[part, 4 * order + side],
                    target,
                )

    def x_end(part, order):
        dzh = turns[order]
        for side in range(WIDE - 1):
            landed(x2_ref.at[part, side, dzh], xb_recv.at[part, 4 * order + side])
        total = add(x2_ref.at[part, 0, dzh], x2_ref.at[part, 1, dzh])
        total += add(x2_ref.at[part, 2, dzh], dense_ref.at[part, dzh, 0])
        sum_ref[part, dzh] = total.astype(jnp.bfloat16)

    def z_begin(part):
        for side, target in enumerate((up, down)):
            push(
                sum_ref.at[part, 2, parts[side]],
                z1_ref.at[part, side],
                zb_send.at[part, side],
                zb_recv.at[part, side],
                target,
            )

    def z_turn(part):
        for side, (dzh, target) in enumerate(((1, up), (3, down))):
            arrival = z1_ref.at[part, side]
            landed(arrival, zb_recv.at[part, side])
            block = sum_ref.at[part, dzh]
            section = block.at[parts[side]]
            section[...] = add(section, arrival).astype(jnp.bfloat16)
            push(
                block,
                z2_ref.at[part, side],
                zb_send.at[part, 2 + side],
                zb_recv.at[part, 2 + side],
                target,
            )

    def z_end(part):
        for side in range(2):
            landed(z2_ref.at[part, side], zb_recv.at[part, 2 + side])
        total = add(z2_ref.at[part, 0], z2_ref.at[part, 1])
        total += sum_ref[part, 0].astype(jnp.float32)
        unpick(owned_ref, part, total.astype(jnp.bfloat16))

    run(back_step, 6, 12)
    sums(0, halves)
    give(0)
    factors()
    collect(1)
    resp_sums(0)

    def write_step(index):
        member, start, lane, column, sign = where_is(index)
        part = pl.ds(start, TILE)
        gq_ref[member, part, :] = (gqf_ref[member, part, :] * gain_ref[core, :1, :]).astype(
            jnp.bfloat16
        )

    run(write_step, 0, count)
    gq_copy = pltpu.make_async_copy(gq_ref, gq_hbm_ref, io_sem.at[1])
    gq_copy.start()
    gain2 = jnp.concatenate([gain[:1], gain[:1]], axis=1)
    for member in range(members):
        for part in range(2):
            unpick(gr_ref.at[member], part, (grf_ref[member, part] * gain2).astype(jnp.bfloat16))
    x_end(1, 0)
    z_begin(1)
    collect(0)
    x_end(1, 1)
    x_end(1, 2)
    z_turn(1)
    x_end(1, 3)
    x_end(0, 0)
    z_begin(0)
    x_end(0, 1)
    x_end(0, 2)
    z_turn(0)
    x_end(0, 3)
    z_end(1)
    z_end(0)
    gq_copy.wait()
    for copy in sent:
        copy.wait_send()


def pair_call(prompt_of, prompt_len, q, own, rkv, w, n_tensor):
    members, rows, hd = q.shape
    block_rows = own.shape[0]
    wide = own.shape[1] // 2
    positions = rkv.shape[1]
    heads = w.shape[0]
    n_prompt, n_resp = 2 * LONG, LONG * WIDE
    span = n_prompt * block_rows
    period = heads * TILE // math.gcd(heads, TILE)
    count = members * rows // TILE
    half = block_rows // 2
    vmem = pl.BlockSpec(memory_space=pltpu.VMEM)
    smem = pl.BlockSpec(memory_space=pltpu.SMEM)
    hbm = pl.BlockSpec(memory_space=pl.ANY)
    dma = pltpu.SemaphoreType.DMA
    low, full = jnp.bfloat16, jnp.float32

    def ways():
        return [dma((2, 4)), dma((2, 4)), dma((2, 16)), dma((2, 16)), dma((2, 8)), dma((2, 8))]

    return pl.pallas_call(
        pair_kernel,
        out_shape=(
            jax.ShapeDtypeStruct((members, rows, hd), low),
            jax.ShapeDtypeStruct((members, positions, 2 * wide), low),
            jax.ShapeDtypeStruct((block_rows, 2 * wide), low),
            jax.ShapeDtypeStruct((1,), full),
        ),
        in_specs=[smem, smem, hbm, vmem, vmem, vmem],
        out_specs=(hbm, vmem, vmem, smem),
        scratch_shapes=[
            pltpu.VMEM((n_resp, block_rows, wide), low),
            pltpu.VMEM((n_resp, block_rows, wide), low),
            pltpu.VMEM((2, n_prompt - 1, block_rows, wide), low),
            pltpu.VMEM((2, span, wide), low),
            pltpu.VMEM((members, rows, hd), low),
            pltpu.VMEM((members, rows, hd), low),
            pltpu.VMEM((period, hd), full),
            pltpu.VMEM((hd, period), full),
            pltpu.VMEM((period, hd), low),
            pltpu.VMEM((hd, period), full),
            pltpu.VMEM((period, wide), low),
            pltpu.VMEM((wide, period), low),
            pltpu.VMEM((members, positions, wide), low),
            pltpu.VMEM((members, positions, wide), low),
            pltpu.VMEM((wide, span), low),
            pltpu.VMEM((wide, span), low),
            pltpu.VMEM((members, wide, positions), low),
            pltpu.VMEM((members, wide, positions), low),
            pltpu.VMEM((span, period), full),
            pltpu.VMEM((members, positions, period), full),
            pltpu.VMEM((span + positions, count * TILE), low),
            pltpu.VMEM((count * TILE, wide), low),
            pltpu.VMEM((count * TILE, wide), low),
            pltpu.VMEM((16, TILE), full),
            pltpu.VMEM((16, TILE), full),
            pltpu.VMEM((8, TILE), full),
            pltpu.VMEM((members, rows, hd), full),
            pltpu.VMEM((n_tensor, 8 * members, hd), full),
            pltpu.VMEM((n_prompt, 8, hd), full),
            pltpu.VMEM((n_prompt * n_resp, hd), full),
            pltpu.VMEM((2, span, wide), low),
            pltpu.VMEM((2, n_prompt, block_rows, wide), low),
            pltpu.VMEM((2, LONG, WIDE, block_rows, wide), low),
            pltpu.VMEM((2, LONG, block_rows, wide), low),
            pltpu.VMEM((members, 2, positions, wide), full),
            pltpu.VMEM((2, WIDE - 1, LONG, block_rows, wide), low),
            pltpu.VMEM((2, 2, half, wide), low),
            pltpu.VMEM((2, 2, block_rows, wide), low),
            *ways(),
            dma((n_tensor - 1,)),
            dma((n_tensor - 1,)),
            dma((n_prompt,)),
            dma((n_prompt,)),
            *ways(),
            dma((2,)),
        ],
        compiler_params=pltpu.CompilerParams(
            collective_id=0, has_side_effects=True, vmem_limit_bytes=56 * 2**20
        ),
    )(prompt_of, prompt_len, q, own, rkv, w)


def shards(queries, resp_kv, prompt_kv, prompt_of, prompt_len, reward_head):
    _, members, positions, heads, hd = queries.shape
    gq, gr, owned, pair_loss = pair_call(
        prompt_of,
        prompt_len,
        queries.reshape(members, positions * heads, hd),
        prompt_kv.reshape(prompt_kv.shape[1], -1),
        resp_kv.reshape(members, positions, -1),
        reward_head,
        lax.axis_size("tensor"),
    )
    return (
        pair_loss,
        gq.reshape(queries.shape),
        gr.reshape(resp_kv.shape),
        owned.reshape(prompt_kv.shape),
    )


def solution(mesh):
    in_specs = (
        P(("prompt", "resp"), None, None, "tensor", None),
        P(("prompt", "resp"), None, None, "tensor", None, None),
        P("resp", "prompt", "tensor", None, None),
        P(),
        P(),
        P("tensor", None),
    )
    out_specs = (
        P(("prompt", "resp")),
        P(("prompt", "resp"), None, None, "tensor", None),
        P(("prompt", "resp"), None, None, "tensor", None, None),
        P("resp", "prompt", "tensor", None, None),
    )
    return jax.shard_map(shards, mesh=mesh, in_specs=in_specs, out_specs=out_specs, check_vma=False)
```

```python
import math

import jax
import jax.numpy as jnp
from jax import lax
from jax.experimental import pallas as pl
from jax.experimental.pallas import tpu as pltpu
from jax.sharding import PartitionSpec as P

BLOCK = 128
TILE = 256

loss_scale = 8192.0


def product(left, right):
    return jnp.dot(left, right, preferred_element_type=jnp.float32)


def product_nt(left, right):
    return lax.dot_general(
        left, right, (((1,), (1,)), ((), ())), preferred_element_type=jnp.float32
    )


LONG = 4
WIDE = 4
MESH = pl.DeviceIdType.MESH


class Place:
    def __init__(self):
        prompt = lax.axis_index("prompt")
        resp = lax.axis_index("resp")
        self.core = lax.rem(prompt, 2)
        self.low = lax.div(prompt, 2)
        self.high = lax.div(resp, WIDE)
        self.x = lax.rem(resp, WIDE)
        self.tensor = lax.axis_index("tensor")
        self.z = self.high * LONG + self.low

    def at(self, dz, dx, core):
        ring = LONG * LONG
        z = lax.rem(self.z + dz + ring, ring)
        x = lax.rem(self.x + dx + WIDE, WIDE)
        return (lax.rem(z, LONG) * 2 + core, lax.div(z, LONG) * WIDE + x, self.tensor)

    def block(self, dz, core):
        return lax.rem(self.low + dz + LONG, LONG) * 2 + core


def remote(src, dst, send, recv, target):
    return pltpu.make_async_remote_copy(
        src_ref=src,
        dst_ref=dst,
        send_sem=send,
        recv_sem=recv,
        device_id=target,
        device_id_type=MESH,
    )


def pair_kernel(
    prompt_of_ref,
    prompt_len_ref,
    q_hbm_ref,
    own_ref,
    rkv_ref,
    w_ref,
    gq_hbm_ref,
    gr_ref,
    owned_ref,
    loss_ref,
    all_k_ref,
    all_v_ref,
    out_ref,
    whole_ref,
    q_ref,
    gq_ref,
    wrow_ref,
    wt_ref,
    mask_ref,
    mask_t_ref,
    w2_ref,
    w2t_ref,
    rk_ref,
    rv_ref,
    kt_ref,
    vt_ref,
    rkt_ref,
    rvt_ref,
    dp_ref,
    drp_ref,
    low_ref,
    ds_ref,
    w2i_ref,
    q2i_ref,
    inverse_ref,
    delta_ref,
    reward_ref,
    gqf_ref,
    vote_ref,
    gain_ref,
    factor_ref,
    piece_ref,
    got_ref,
    dense_ref,
    sum_ref,
    grf_ref,
    x2_ref,
    z1_ref,
    z2_ref,
    z_send,
    z_recv,
    x_send,
    x_recv,
    c_send,
    c_recv,
    y_send,
    y_recv,
    g_send,
    g_recv,
    zb_send,
    zb_recv,
    xb_send,
    xb_recv,
    cb_send,
    cb_recv,
    io_sem,
):
    members, rows, hd = q_ref.shape
    block_rows = own_ref.shape[0]
    span = whole_ref.shape[1]
    positions = rkv_ref.shape[1]
    heads = w_ref.shape[0]
    blocks = span // BLOCK
    period = wrow_ref.shape[0]
    phases = period // TILE
    tiles = rows // TILE
    wide = 2 * hd
    scale = hd**-0.5
    pace = scale * math.log2(math.e)
    n_resp = LONG * WIDE
    n_tensor = vote_ref.shape[0]
    count = members * tiles
    keys = pl.ds(0, span)
    tail = pl.ds(span, positions)

    def unpick(ref, part, value):
        for g in range(2):
            low = (2 * g + part) * hd
            ref[:, low : low + hd] = value[:, g * hd : (g + 1) * hd]

    q_copy = pltpu.make_async_copy(q_hbm_ref, q_ref, io_sem.at[0])
    q_copy.start()
    me = Place()
    core = me.core
    half = block_rows // 2
    parts = (pl.ds(0, half), pl.ds(half, half))
    up, down = me.at(LONG, 0, core), me.at(-LONG, 0, core)
    right, left = me.at(0, 1, core), me.at(0, -1, core)
    across = me.at(0, 2, core)
    sides = (right, left, across)
    far = 2 - 4 * core
    here = me.at(0, 0, core)
    peers = [
        (here[0], here[1], lax.rem(me.tensor + step, n_tensor)) for step in range(1, n_tensor)
    ]
    barrier = pltpu.get_barrier_semaphore()
    friends = (
        [up, down, right, left, me.at(0, 0, 1 - core)]
        + [me.at(dz, 0, c) for dz in (1, -1) for c in range(2)]
        + [me.at(-2, 0, 0), me.at(2, 0, 1), me.at(far, 0, core)]
        + [across]
        + peers
    )
    for device in friends:
        pl.semaphore_signal(barrier, inc=1, device_id=device, device_id_type=MESH)
    pl.semaphore_wait(barrier, len(friends))

    sent = []

    def push(src, dst, send, recv, target):
        copy = remote(src, dst, send, recv, target)
        copy.start()
        sent.append(copy)

    def landed(ref, recv):
        remote(ref, ref, y_send.at[0], recv, up).wait_recv()

    def slot(dzh, dx):
        return lax.rem(me.high + dzh + LONG, LONG) * WIDE + lax.rem(me.x + dx + WIDE, WIDE)

    tables = (all_k_ref, all_v_ref)

    def spread(part, order, dzh):
        block = tables[part].at[slot(dzh, 0)]
        for side, target in enumerate(sides):
            index = 4 * order + side
            push(block, block, x_send.at[part, index], x_recv.at[part, index], target)

    def begin(part):
        mine = slot(0, 0)
        for g in range(2):
            tables[part][mine, :, g * hd : (g + 1) * hd] = own_ref[:, g, part, :]
        block = tables[part].at[slot(0, 0)]
        push(block, block, z_send.at[part, 0], z_recv.at[part, 0], up)
        push(block, block, z_send.at[part, 1], z_recv.at[part, 1], down)
        spread(part, 0, 0)

    def turn(part):
        for side, (dzh, target) in enumerate(((-1, up), (1, down))):
            block = tables[part].at[slot(dzh, 0)]
            landed(block, z_recv.at[part, side])
            section = block.at[parts[side]]
            push(section, section, z_send.at[part, 2 + side], z_recv.at[part, 2 + side], target)

    def middle(part):
        spread(part, 1, -1)
        spread(part, 2, 1)

    def opposite(part):
        block = tables[part].at[slot(2, 0)]
        for side in range(2):
            landed(block.at[parts[side]], z_recv.at[part, 2 + side])
        spread(part, 3, 2)

    def complete(part):
        for order, dzh in enumerate((0, -1, 1, 2)):
            for side, dx in enumerate((-1, 1, 2)):
                landed(tables[part].at[slot(dzh, dx)], x_recv.at[part, 4 * order + side])

    def place(device_block):
        return pl.ds(pl.multiple_of(device_block * block_rows, block_rows), block_rows)

    def name(device):
        return prompt_of_ref[device[0] * n_resp + device[1]]

    def deliver(part):
        mine = whole_ref.at[part, place(me.block(0, core))]
        index = 0
        for kind, dz in ((3, far), (1, 1), (2, -1), (0, 0)):
            for c in range(2) if kind else (1 - core,):
                target = me.at(dz, 0, c)
                out_ref[part, index] = tables[part][name(target)]
                push(
                    out_ref.at[part, index],
                    mine,
                    c_send.at[part, index],
                    c_recv.at[part, 2 * kind + core],
                    target,
                )
                index += 1
        mine[...] = tables[part][name(here)]

    def receive(part):
        for kind, dz in ((0, 0), (1, -1), (2, 1), (3, 2)):
            for c in range(2) if kind else (1 - core,):
                landed(whole_ref.at[part, place(me.block(dz, c))], c_recv.at[part, 2 * kind + c])

    begin(0)

    for index in range(period // heads):
        wrow_ref[index * heads : (index + 1) * heads, :] = w_ref[...]
    for phase in range(phases):
        part = slice(phase * TILE, (phase + 1) * TILE)
        row = lax.broadcasted_iota(jnp.int32, (TILE, hd), 0) + phase * TILE
        first = (lax.rem(row, heads) < heads // 2).astype(jnp.float32)
        wrow = wrow_ref[part, :]
        mask_ref[part, :] = first.astype(jnp.bfloat16)
        mask_t_ref[:, part] = first.T
        wt_ref[:, part] = wrow.T
        w2 = jnp.concatenate([wrow * first, wrow * (1.0 - first)], axis=1)
        w2_ref[part, :] = w2.astype(jnp.bfloat16)
        w2t_ref[:, part] = w2.T.astype(jnp.bfloat16)
    for member in range(members):
        for g in range(2):
            low = slice(g * hd, (g + 1) * hd)
            rk_ref[member, :, low] = rkv_ref[member, :, g, 0, :]
            rv_ref[member, :, low] = rkv_ref[member, :, g, 1, :]
        rkt_ref[member] = rk_ref[member].astype(jnp.float32).T.astype(jnp.bfloat16)
        rvt_ref[member] = rv_ref[member].astype(jnp.float32).T.astype(jnp.bfloat16)
        drp_ref[member] = product(rv_ref[member], w2t_ref[...])
    reward_ref[...] = jnp.zeros_like(reward_ref)

    turn(0)
    begin(1)
    middle(0)
    opposite(0)
    turn(1)
    middle(1)
    complete(0)
    deliver(0)
    opposite(1)
    complete(1)
    deliver(1)

    length = prompt_len_ref[name(here)]
    shades = [jnp.where(block < length, 0.0, -1e30) for block in range(blocks)]
    strips = [slice(block * BLOCK, (block + 1) * BLOCK) for block in range(blocks)]

    PAIRED = 2

    def where_is(index):
        member = lax.div(index, tiles)
        start = pl.multiple_of(lax.rem(index, tiles) * TILE, TILE)
        lane = pl.ds(pl.multiple_of(lax.rem(index, phases) * TILE, TILE), TILE)
        column = pl.ds(pl.multiple_of(index * TILE, TILE), TILE)
        sign = (2 * member - 1).astype(jnp.float32)
        return member, start, lane, column, sign

    def paired(step):
        def body(index, carry):
            for sub in range(PAIRED):
                step(index * PAIRED + sub)
            return carry

        return body

    def run(step, first, last):
        lax.fori_loop(first // PAIRED, last // PAIRED, paired(step), 0)

    wider = 2 * BLOCK
    broad = [slice(start, start + wider) for start in range(0, span, wider)]

    def score_step(index):
        member, start, lane, column, sign = where_is(index)
        q = q_ref[member, pl.ds(start, TILE), :]
        first = mask_ref[lane, :]
        q2 = jnp.concatenate([q * first, q * (1 - first)], axis=1)
        sr = product_nt(rk_ref[member], q2)
        causal = (
            lax.broadcasted_iota(jnp.int32, (positions, TILE), 0) * heads
            <= lax.broadcasted_iota(jnp.int32, (positions, TILE), 1) + start
        )
        sr = jnp.where(causal, sr, -1e30)
        highest = jnp.max(sr, axis=0, keepdims=True)
        for number, part in enumerate(broad):
            s = product_nt(whole_ref[0, part, :], q2)
            for sub in range(2):
                top = jnp.max(s[sub * BLOCK : (sub + 1) * BLOCK], axis=0, keepdims=True)
                highest = jnp.maximum(highest, top + shades[2 * number + sub])
        er = jnp.exp2((sr - highest) * pace)
        total = jnp.sum(er, axis=0, keepdims=True)
        low_ref[tail, column] = er.astype(jnp.bfloat16)
        for number, part in enumerate(broad):
            s = product_nt(whole_ref[0, part, :], q2)
            for sub in range(2):
                shifted = s[sub * BLOCK : (sub + 1) * BLOCK] - (highest - shades[2 * number + sub])
                e = jnp.exp2(shifted * pace)
                total = total + jnp.sum(e, axis=0, keepdims=True)
                low_ref[strips[2 * number + sub], column] = e.astype(jnp.bfloat16)
        inverse = 1.0 / total
        inverse_ref[pl.ds(index, 1), :] = inverse
        turned = jnp.broadcast_to(inverse * sign, (hd, TILE)).T
        qi = q.astype(jnp.float32) * turned
        wi = wrow_ref[lane, :].astype(jnp.bfloat16).astype(jnp.float32) * turned
        firstf = first.astype(jnp.float32)
        q2i_ref[column, :] = jnp.concatenate([qi * firstf, qi * (1 - firstf)], axis=1).astype(
            jnp.bfloat16
        )
        w2i_ref[column, :] = jnp.concatenate([wi * firstf, wi * (1 - firstf)], axis=1).astype(
            jnp.bfloat16
        )

    def out_step(index):
        member, start, lane, column, sign = where_is(index)
        both = product(vt_ref[...], low_ref[keys, column])
        both += product(rvt_ref[member], low_ref[tail, column])
        out = jnp.where(mask_t_ref[:, lane] > 0.5, both[:hd], both[hd:])
        out = (out * inverse_ref[pl.ds(index, 1), :]).astype(jnp.bfloat16).astype(jnp.float32)
        wt = wt_ref[:, lane]
        reward_ref[pl.ds(member, 1), :] += jnp.sum(out * wt, axis=0, keepdims=True)
        delta_ref[pl.ds(index, 1), :] = jnp.sum(
            out * wt.astype(jnp.bfloat16).astype(jnp.float32), axis=0, keepdims=True
        )

    def back_step(index):
        member, start, lane, column, sign = where_is(index)
        delta = delta_ref[pl.ds(index, 1), :]
        ds = jnp.concatenate(
            [
                low_ref[strip, column] * (dp_ref[strip, lane] - delta).astype(jnp.bfloat16)
                for strip in strips
            ],
            axis=0,
        )
        dsr = low_ref[tail, column] * (drp_ref[member, :, lane] - delta).astype(jnp.bfloat16)
        ds_ref[keys, column] = ds
        ds_ref[tail, column] = dsr
        both = product(kt_ref[...], ds) + product(rkt_ref[member], dsr)
        gq = jnp.where(mask_t_ref[:, lane] > 0.5, both[:hd], both[hd:])
        gq = gq * (inverse_ref[pl.ds(index, 1), :] * (sign * scale))
        gqf_ref[member, pl.ds(start, TILE), :] = gq.T

    def resp_sums(part):
        left_ref, right_ref = ((ds_ref, q2i_ref), (low_ref, w2i_ref))[part]
        factor = 1.0 if part else scale
        for member in range(members):
            column = slice(member * rows, (member + 1) * rows)
            grf_ref[member, part] = product(left_ref[tail, column], right_ref[column, :]) * factor

    def sums(part):
        left_ref, right_ref = ((ds_ref, q2i_ref), (low_ref, w2i_ref))[part]
        factor = 1.0 if part else scale
        for kind, dz in ((3, 2), (1, 1), (2, -1), (0, 0)):
            row = pl.ds(pl.multiple_of(me.block(dz, 0) * block_rows, block_rows), 2 * block_rows)
            value = product(left_ref[row, :], right_ref[...]) * factor
            piece_ref[part, row, :] = value.astype(jnp.bfloat16)
            yield kind, dz

    def give(part, ready):
        index = 0
        for kind, dz in ready:
            for c in range(2) if kind else (1 - core,):
                push(
                    piece_ref.at[part, place(me.block(dz, c))],
                    got_ref.at[part, 2 * kind + core],
                    cb_send.at[part, index],
                    cb_recv.at[part, 2 * kind + core],
                    me.at(dz if kind != 3 else 4 * c - 2, 0, c),
                )
                index += 1
        got_ref[part, core] = piece_ref[part, place(me.block(0, core)), :]

    receive(0)
    for strip in strips:
        kt_ref[:, strip] = whole_ref[0, strip, :].astype(jnp.float32).T.astype(jnp.bfloat16)
    q_copy.wait()
    run(score_step, 0, count)
    value_pieces = list(sums(1))
    receive(1)
    give(1, value_pieces)
    for strip in strips:
        vt_ref[:, strip] = whole_ref[1, strip, :].astype(jnp.float32).T.astype(jnp.bfloat16)
    run(out_step, 0, count)

    ballot = vote_ref.at[me.tensor]
    for member in range(members):
        total = jnp.sum(reward_ref[member : member + 1, :], axis=1, keepdims=True)
        ballot[8 * member : 8 * (member + 1), :] = jnp.broadcast_to(total, (8, hd))
    for step, target in enumerate(peers):
        push(ballot, ballot, y_send.at[step], y_recv.at[step], target)
    dp_ref[...] = product(whole_ref[1], w2t_ref[...])
    run(back_step, 0, 6)

    for step in range(1, n_tensor):
        source = lax.rem(me.tensor + n_tensor - step, n_tensor)
        landed(vote_ref.at[source], y_recv.at[step - 1])
    reward = vote_ref[0]
    for index in range(1, n_tensor):
        reward = reward + vote_ref[index]
    reward = reward / positions
    margin = reward[8:16] - reward[:8]
    tiny = jnp.exp(-jnp.abs(margin))
    loss = jnp.maximum(margin, 0.0) + jnp.log1p(tiny)
    loss_ref[0] = loss[0, 0]
    sigmoid_gap = jnp.where(margin >= 0.0, 1.0, tiny) / (1.0 + tiny)
    gain = sigmoid_gap * (loss_scale / positions)
    gain_ref[core] = gain
    index = 0
    for kind, dz in ((3, 2), (1, 1), (2, -1), (0, 0)):
        for c in range(2) if kind else (1 - core,):
            push(
                gain_ref.at[core],
                gain_ref.at[2 * kind + core],
                g_send.at[index],
                g_recv.at[2 * kind + core],
                me.at(dz if kind != 3 else 4 * c - 2, 0, c),
            )
            index += 1

    names = [
        name(me.at(dz, 0, c)) for kind, dz in ((0, 0), (1, -1), (2, 1), (3, far)) for c in range(2)
    ]
    chunk = 16
    lanes = 128
    turns = (2, 1, 3, 0)
    sources = len(names)

    def factors():
        for kind in range(4):
            for c in range(2) if kind else (1 - core,):
                landed(gain_ref.at[2 * kind + c], g_recv.at[2 * kind + c])
        for a in range(LONG):
            for b in range(WIDE):
                prompt = slot(a, b)
                for source in range(sources):
                    row = (a * WIDE + b) * sources + source
                    share = jnp.where(names[source] == prompt, 1.0, 0.0)
                    factor_ref[row : row + 1, :] = gain_ref[source, :1, :] * share

    def add(left_ref, right_ref):
        return left_ref[...].astype(jnp.float32) + right_ref[...].astype(jnp.float32)

    def collect(part):
        for kind in range(4):
            for c in range(2) if kind else (1 - core,):
                landed(got_ref.at[part, 2 * kind + c], cb_recv.at[part, 2 * kind + c])

        for order, dzh in enumerate(turns):

            def select(index, carry):
                row = pl.ds(pl.multiple_of(index * chunk, chunk), chunk)
                for start in range(0, wide, lanes):
                    column = slice(start, start + lanes)
                    terms = [
                        got_ref[part, source, row, column].astype(jnp.float32)
                        for source in range(sources)
                    ]
                    for b in range(WIDE):
                        base = (dzh * WIDE + b) * sources
                        total = terms[0] * factor_ref[base : base + 1, :]
                        for source in range(1, sources):
                            at = base + source
                            total += terms[source] * factor_ref[at : at + 1, :]
                        dense_ref[part, dzh, b, row, column] = total.astype(jnp.bfloat16)
                return carry

            lax.fori_loop(0, block_rows // chunk, select, 0)
            for side, (dx, target) in enumerate(zip((1, 3, 2), sides)):
                push(
                    dense_ref.at[part, dzh, dx],
                    x2_ref.at[part, side, dzh],
                    xb_send.at[part, 4 * order + side],
                    xb_recv.at[part, 4 * order + side],
                    target,
                )

    def x_end(part, order):
        dzh = turns[order]
        for side in range(WIDE - 1):
            landed(x2_ref.at[part, side, dzh], xb_recv.at[part, 4 * order + side])
        total = add(x2_ref.at[part, 0, dzh], x2_ref.at[part, 1, dzh])
        total += add(x2_ref.at[part, 2, dzh], dense_ref.at[part, dzh, 0])
        sum_ref[part, dzh] = total.astype(jnp.bfloat16)

    def z_begin(part):
        for side, target in enumerate((up, down)):
            push(
                sum_ref.at[part, 2, parts[side]],
                z1_ref.at[part, side],
                zb_send.at[part, side],
                zb_recv.at[part, side],
                target,
            )

    def z_turn(part):
        for side, (dzh, target) in enumerate(((1, up), (3, down))):
            arrival = z1_ref.at[part, side]
            landed(arrival, zb_recv.at[part, side])
            block = sum_ref.at[part, dzh]
            section = block.at[parts[side]]
            section[...] = add(section, arrival).astype(jnp.bfloat16)
            push(
                block,
                z2_ref.at[part, side],
                zb_send.at[part, 2 + side],
                zb_recv.at[part, 2 + side],
                target,
            )

    def z_end(part):
        for side in range(2):
            landed(z2_ref.at[part, side], zb_recv.at[part, 2 + side])
        total = add(z2_ref.at[part, 0], z2_ref.at[part, 1])
        total += sum_ref[part, 0].astype(jnp.float32)
        unpick(owned_ref, part, total.astype(jnp.bfloat16))

    run(back_step, 6, 12)
    give(0, sums(0))
    factors()
    collect(1)
    resp_sums(0)
    resp_sums(1)

    def write_step(index):
        member, start, lane, column, sign = where_is(index)
        part = pl.ds(start, TILE)
        gq_ref[member, part, :] = (gqf_ref[member, part, :] * gain_ref[core, :1, :]).astype(
            jnp.bfloat16
        )

    run(write_step, 0, count)
    gq_copy = pltpu.make_async_copy(gq_ref, gq_hbm_ref, io_sem.at[1])
    gq_copy.start()
    gain2 = jnp.concatenate([gain[:1], gain[:1]], axis=1)
    for member in range(members):
        pair = [(grf_ref[member, part] * gain2).astype(jnp.bfloat16) for part in range(2)]
        for g in range(2):
            low = slice(g * hd, (g + 1) * hd)
            gr_ref[member, :, g, :, :] = jnp.stack([each[:, low] for each in pair], axis=1)
    x_end(1, 0)
    z_begin(1)
    collect(0)
    x_end(1, 1)
    x_end(1, 2)
    z_turn(1)
    x_end(1, 3)
    x_end(0, 0)
    z_begin(0)
    x_end(0, 1)
    x_end(0, 2)
    z_turn(0)
    x_end(0, 3)
    z_end(1)
    z_end(0)
    gq_copy.wait()
    for copy in sent:
        copy.wait_send()


def pair_call(prompt_of, prompt_len, q, own, rkv, w, n_tensor):
    members, rows, hd = q.shape
    block_rows = own.shape[0]
    wide = 2 * hd
    positions = rkv.shape[1]
    heads = w.shape[0]
    n_prompt, n_resp = 2 * LONG, LONG * WIDE
    span = n_prompt * block_rows
    period = heads * TILE // math.gcd(heads, TILE)
    count = members * rows // TILE
    half = block_rows // 2
    vmem = pl.BlockSpec(memory_space=pltpu.VMEM)
    smem = pl.BlockSpec(memory_space=pltpu.SMEM)
    hbm = pl.BlockSpec(memory_space=pl.ANY)
    dma = pltpu.SemaphoreType.DMA
    low, full = jnp.bfloat16, jnp.float32

    def ways():
        return [dma((2, 4)), dma((2, 4)), dma((2, 16)), dma((2, 16)), dma((2, 8)), dma((2, 8))]

    return pl.pallas_call(
        pair_kernel,
        out_shape=(
            jax.ShapeDtypeStruct((members, rows, hd), low),
            jax.ShapeDtypeStruct((members, positions, 2, 2, hd), low),
            jax.ShapeDtypeStruct((block_rows, 2 * wide), low),
            jax.ShapeDtypeStruct((1,), full),
        ),
        in_specs=[smem, smem, hbm, vmem, vmem, vmem],
        out_specs=(hbm, vmem, vmem, smem),
        scratch_shapes=[
            pltpu.VMEM((n_resp, block_rows, wide), low),
            pltpu.VMEM((n_resp, block_rows, wide), low),
            pltpu.VMEM((2, n_prompt - 1, block_rows, wide), low),
            pltpu.VMEM((2, span, wide), low),
            pltpu.VMEM((members, rows, hd), low),
            pltpu.VMEM((members, rows, hd), low),
            pltpu.VMEM((period, hd), full),
            pltpu.VMEM((hd, period), full),
            pltpu.VMEM((period, hd), low),
            pltpu.VMEM((hd, period), full),
            pltpu.VMEM((period, wide), low),
            pltpu.VMEM((wide, period), low),
            pltpu.VMEM((members, positions, wide), low),
            pltpu.VMEM((members, positions, wide), low),
            pltpu.VMEM((wide, span), low),
            pltpu.VMEM((wide, span), low),
            pltpu.VMEM((members, wide, positions), low),
            pltpu.VMEM((members, wide, positions), low),
            pltpu.VMEM((span, period), full),
            pltpu.VMEM((members, positions, period), full),
            pltpu.VMEM((span + positions, count * TILE), low),
            pltpu.VMEM((span + positions, count * TILE), low),
            pltpu.VMEM((count * TILE, wide), low),
            pltpu.VMEM((count * TILE, wide), low),
            pltpu.VMEM((16, TILE), full),
            pltpu.VMEM((16, TILE), full),
            pltpu.VMEM((8, TILE), full),
            pltpu.VMEM((members, rows, hd), full),
            pltpu.VMEM((n_tensor, 8 * members, hd), full),
            pltpu.VMEM((n_prompt, 8, hd), full),
            pltpu.VMEM((n_prompt * n_resp, hd), full),
            pltpu.VMEM((2, span, wide), low),
            pltpu.VMEM((2, n_prompt, block_rows, wide), low),
            pltpu.VMEM((2, LONG, WIDE, block_rows, wide), low),
            pltpu.VMEM((2, LONG, block_rows, wide), low),
            pltpu.VMEM((members, 2, positions, wide), full),
            pltpu.VMEM((2, WIDE - 1, LONG, block_rows, wide), low),
            pltpu.VMEM((2, 2, half, wide), low),
            pltpu.VMEM((2, 2, block_rows, wide), low),
            *ways(),
            dma((n_tensor - 1,)),
            dma((n_tensor - 1,)),
            dma((n_prompt,)),
            dma((n_prompt,)),
            *ways(),
            dma((2,)),
        ],
        compiler_params=pltpu.CompilerParams(
            collective_id=0, has_side_effects=True, vmem_limit_bytes=56 * 2**20
        ),
    )(prompt_of, prompt_len, q, own, rkv, w)


def shards(queries, resp_kv, prompt_kv, prompt_of, prompt_len, reward_head):
    _, members, positions, heads, hd = queries.shape
    gq, gr, owned, pair_loss = pair_call(
        prompt_of,
        prompt_len,
        queries.reshape(members, positions * heads, hd),
        prompt_kv[0],
        resp_kv[0],
        reward_head,
        lax.axis_size("tensor"),
    )
    return (
        pair_loss,
        gq.reshape(queries.shape),
        gr.reshape(resp_kv.shape),
        owned.reshape(prompt_kv.shape),
    )


def solution(mesh):
    in_specs = (
        P(("prompt", "resp"), None, None, "tensor", None),
        P(("prompt", "resp"), None, None, "tensor", None, None),
        P("resp", "prompt", "tensor", None, None),
        P(),
        P(),
        P("tensor", None),
    )
    out_specs = (
        P(("prompt", "resp")),
        P(("prompt", "resp"), None, None, "tensor", None),
        P(("prompt", "resp"), None, None, "tensor", None, None),
        P("resp", "prompt", "tensor", None, None),
    )
    return jax.shard_map(shards, mesh=mesh, in_specs=in_specs, out_specs=out_specs, check_vma=False)
```

```python
import math

import jax
import jax.numpy as jnp
from jax import lax
from jax.experimental import pallas as pl
from jax.experimental.pallas import tpu as pltpu
from jax.sharding import PartitionSpec as P

BLOCK = 128
TILE = 256

loss_scale = 8192.0


def product(left, right):
    return jnp.dot(left, right, preferred_element_type=jnp.float32)


def product_nt(left, right):
    return lax.dot_general(
        left, right, (((1,), (1,)), ((), ())), preferred_element_type=jnp.float32
    )


LONG = 4
WIDE = 4
MESH = pl.DeviceIdType.MESH


class Place:
    def __init__(self):
        prompt = lax.axis_index("prompt")
        resp = lax.axis_index("resp")
        self.core = lax.rem(prompt, 2)
        self.low = lax.div(prompt, 2)
        self.high = lax.div(resp, WIDE)
        self.x = lax.rem(resp, WIDE)
        self.tensor = lax.axis_index("tensor")
        self.z = self.high * LONG + self.low

    def at(self, dz, dx, core):
        ring = LONG * LONG
        z = lax.rem(self.z + dz + ring, ring)
        x = lax.rem(self.x + dx + WIDE, WIDE)
        return (lax.rem(z, LONG) * 2 + core, lax.div(z, LONG) * WIDE + x, self.tensor)

    def block(self, dz, core):
        return lax.rem(self.low + dz + LONG, LONG) * 2 + core


def remote(src, dst, send, recv, target):
    return pltpu.make_async_remote_copy(
        src_ref=src,
        dst_ref=dst,
        send_sem=send,
        recv_sem=recv,
        device_id=target,
        device_id_type=MESH,
    )


def pair_kernel(
    prompt_of_ref,
    prompt_len_ref,
    q_hbm_ref,
    own_ref,
    rkv_ref,
    w_ref,
    gq_hbm_ref,
    gr_ref,
    owned_ref,
    loss_ref,
    all_k_ref,
    all_v_ref,
    out_ref,
    whole_ref,
    q_ref,
    gq_ref,
    wrow_ref,
    wt_ref,
    mask_ref,
    mask_t_ref,
    w2_ref,
    w2t_ref,
    rk_ref,
    rv_ref,
    kt_ref,
    vt_ref,
    rkt_ref,
    rvt_ref,
    dp_ref,
    drp_ref,
    low_ref,
    ds_ref,
    w2i_ref,
    q2i_ref,
    inverse_ref,
    delta_ref,
    reward_ref,
    gqf_ref,
    vote_ref,
    gain_ref,
    factor_ref,
    piece_ref,
    got_ref,
    dense_ref,
    sum_ref,
    grf_ref,
    x2_ref,
    z1_ref,
    z2_ref,
    z_send,
    z_recv,
    x_send,
    x_recv,
    c_send,
    c_recv,
    y_send,
    y_recv,
    g_send,
    g_recv,
    zb_send,
    zb_recv,
    xb_send,
    xb_recv,
    cb_send,
    cb_recv,
    io_sem,
):
    members, rows, hd = q_ref.shape
    block_rows = own_ref.shape[0]
    span = whole_ref.shape[1]
    positions = rkv_ref.shape[1]
    heads = w_ref.shape[0]
    blocks = span // BLOCK
    period = wrow_ref.shape[0]
    phases = period // TILE
    tiles = rows // TILE
    wide = 2 * hd
    scale = hd**-0.5
    pace = scale * math.log2(math.e)
    n_resp = LONG * WIDE
    n_tensor = vote_ref.shape[0]
    count = members * tiles
    keys = pl.ds(0, span)
    tail = pl.ds(span, positions)

    q_copy = pltpu.make_async_copy(q_hbm_ref, q_ref, io_sem.at[0])
    q_copy.start()
    me = Place()
    core = me.core
    half = block_rows // 2
    parts = (pl.ds(0, half), pl.ds(half, half))
    up, down = me.at(LONG, 0, core), me.at(-LONG, 0, core)
    right, left = me.at(0, 1, core), me.at(0, -1, core)
    across = me.at(0, 2, core)
    sides = (right, left, across)
    far = 2 - 4 * core
    here = me.at(0, 0, core)
    peers = [
        (here[0], here[1], lax.rem(me.tensor + step, n_tensor)) for step in range(1, n_tensor)
    ]
    barrier = pltpu.get_barrier_semaphore()
    friends = (
        [up, down, right, left, me.at(0, 0, 1 - core)]
        + [me.at(dz, 0, c) for dz in (1, -1) for c in range(2)]
        + [me.at(-2, 0, 0), me.at(2, 0, 1), me.at(far, 0, core)]
        + [across]
        + peers
    )
    for device in friends:
        pl.semaphore_signal(barrier, inc=1, device_id=device, device_id_type=MESH)
    pl.semaphore_wait(barrier, len(friends))

    sent = []

    def push(src, dst, send, recv, target):
        copy = remote(src, dst, send, recv, target)
        copy.start()
        sent.append(copy)

    def landed(ref, recv):
        remote(ref, ref, y_send.at[0], recv, up).wait_recv()

    def slot(dzh, dx):
        return lax.rem(me.high + dzh + LONG, LONG) * WIDE + lax.rem(me.x + dx + WIDE, WIDE)

    tables = (all_k_ref, all_v_ref)

    def spread(part, order, dzh):
        block = tables[part].at[slot(dzh, 0)]
        for side, target in enumerate(sides):
            index = 4 * order + side
            push(block, block, x_send.at[part, index], x_recv.at[part, index], target)

    def begin(part):
        mine = slot(0, 0)
        for g in range(2):
            tables[part][mine, :, g * hd : (g + 1) * hd] = own_ref[:, g, part, :]
        block = tables[part].at[slot(0, 0)]
        push(block, block, z_send.at[part, 0], z_recv.at[part, 0], up)
        push(block, block, z_send.at[part, 1], z_recv.at[part, 1], down)
        spread(part, 0, 0)

    def turn(part):
        for side, (dzh, target) in enumerate(((-1, up), (1, down))):
            block = tables[part].at[slot(dzh, 0)]
            landed(block, z_recv.at[part, side])
            section = block.at[parts[side]]
            push(section, section, z_send.at[part, 2 + side], z_recv.at[part, 2 + side], target)

    def middle(part):
        spread(part, 1, -1)
        spread(part, 2, 1)

    def opposite(part):
        block = tables[part].at[slot(2, 0)]
        for side in range(2):
            landed(block.at[parts[side]], z_recv.at[part, 2 + side])
        spread(part, 3, 2)

    def complete(part):
        for order, dzh in enumerate((0, -1, 1, 2)):
            for side, dx in enumerate((-1, 1, 2)):
                landed(tables[part].at[slot(dzh, dx)], x_recv.at[part, 4 * order + side])

    def place(device_block):
        return pl.ds(pl.multiple_of(device_block * block_rows, block_rows), block_rows)

    def name(device):
        return prompt_of_ref[device[0] * n_resp + device[1]]

    def deliver(part):
        mine = whole_ref.at[part, place(me.block(0, core))]
        index = 0
        for kind, dz in ((3, far), (1, 1), (2, -1), (0, 0)):
            for c in range(2) if kind else (1 - core,):
                target = me.at(dz, 0, c)
                out_ref[part, index] = tables[part][name(target)]
                push(
                    out_ref.at[part, index],
                    mine,
                    c_send.at[part, index],
                    c_recv.at[part, 2 * kind + core],
                    target,
                )
                index += 1
        mine[...] = tables[part][name(here)]

    def receive(part):
        for kind, dz in ((0, 0), (1, -1), (2, 1), (3, 2)):
            for c in range(2) if kind else (1 - core,):
                landed(whole_ref.at[part, place(me.block(dz, c))], c_recv.at[part, 2 * kind + c])

    begin(0)

    for index in range(period // heads):
        wrow_ref[index * heads : (index + 1) * heads, :] = w_ref[...]
    for phase in range(phases):
        part = slice(phase * TILE, (phase + 1) * TILE)
        row = lax.broadcasted_iota(jnp.int32, (TILE, hd), 0) + phase * TILE
        first = (lax.rem(row, heads) < heads // 2).astype(jnp.float32)
        wrow = wrow_ref[part, :]
        mask_ref[part, :] = first.astype(jnp.bfloat16)
        mask_t_ref[:, part] = first.T
        wt_ref[:, part] = wrow.T
        w2 = jnp.concatenate([wrow * first, wrow * (1.0 - first)], axis=1)
        w2_ref[part, :] = w2.astype(jnp.bfloat16)
        w2t_ref[:, part] = w2.T.astype(jnp.bfloat16)
    for member in range(members):
        for g in range(2):
            low = slice(g * hd, (g + 1) * hd)
            rk_ref[member, :, low] = rkv_ref[member, :, g, 0, :]
            rv_ref[member, :, low] = rkv_ref[member, :, g, 1, :]
        rkt_ref[member] = rk_ref[member].astype(jnp.float32).T.astype(jnp.bfloat16)
        rvt_ref[member] = rv_ref[member].astype(jnp.float32).T.astype(jnp.bfloat16)
        drp_ref[member] = product(rv_ref[member], w2t_ref[...])
    reward_ref[...] = jnp.zeros_like(reward_ref)

    turn(0)
    begin(1)
    middle(0)
    opposite(0)
    turn(1)
    middle(1)
    complete(0)
    deliver(0)
    opposite(1)
    complete(1)
    deliver(1)

    length = prompt_len_ref[name(here)]
    shades = [jnp.where(block < length, 0.0, -1e30) for block in range(blocks)]
    strips = [slice(block * BLOCK, (block + 1) * BLOCK) for block in range(blocks)]

    PAIRED = 2

    def where_is(index):
        member = lax.div(index, tiles)
        start = pl.multiple_of(lax.rem(index, tiles) * TILE, TILE)
        lane = pl.ds(pl.multiple_of(lax.rem(index, phases) * TILE, TILE), TILE)
        column = pl.ds(pl.multiple_of(index * TILE, TILE), TILE)
        sign = (2 * member - 1).astype(jnp.float32)
        return member, start, lane, column, sign

    def paired(step):
        def body(index, carry):
            for sub in range(PAIRED):
                step(index * PAIRED + sub)
            return carry

        return body

    def run(step, first, last):
        lax.fori_loop(first // PAIRED, last // PAIRED, paired(step), 0)

    wider = 2 * BLOCK
    broad = [slice(start, start + wider) for start in range(0, span, wider)]

    def score_step(index):
        member, start, lane, column, sign = where_is(index)
        q = q_ref[member, pl.ds(start, TILE), :]
        first = mask_ref[lane, :]
        q2 = jnp.concatenate([q * first, q * (1 - first)], axis=1)
        sr = product_nt(rk_ref[member], q2)
        causal = (
            lax.broadcasted_iota(jnp.int32, (positions, TILE), 0) * heads
            <= lax.broadcasted_iota(jnp.int32, (positions, TILE), 1) + start
        )
        sr = jnp.where(causal, sr, -1e30)
        highest = jnp.max(sr, axis=0, keepdims=True)
        for number, part in enumerate(broad):
            s = product_nt(whole_ref[0, part, :], q2)
            for sub in range(2):
                top = jnp.max(s[sub * BLOCK : (sub + 1) * BLOCK], axis=0, keepdims=True)
                highest = jnp.maximum(highest, top + shades[2 * number + sub])
        er = jnp.exp2((sr - highest) * pace)
        total = jnp.sum(er, axis=0, keepdims=True)
        low_ref[tail, column] = er.astype(jnp.bfloat16)
        for number, part in enumerate(broad):
            s = product_nt(whole_ref[0, part, :], q2)
            for sub in range(2):
                shifted = s[sub * BLOCK : (sub + 1) * BLOCK] - (highest - shades[2 * number + sub])
                e = jnp.exp2(shifted * pace)
                total = total + jnp.sum(e, axis=0, keepdims=True)
                low_ref[strips[2 * number + sub], column] = e.astype(jnp.bfloat16)
        inverse = 1.0 / total
        inverse_ref[pl.ds(index, 1), :] = inverse
        turned = jnp.broadcast_to(inverse * sign, (hd, TILE)).T
        qi = q.astype(jnp.float32) * turned
        wi = wrow_ref[lane, :].astype(jnp.bfloat16).astype(jnp.float32) * turned
        firstf = first.astype(jnp.float32)
        q2i_ref[column, :] = jnp.concatenate([qi * firstf, qi * (1 - firstf)], axis=1).astype(
            jnp.bfloat16
        )
        w2i_ref[column, :] = jnp.concatenate([wi * firstf, wi * (1 - firstf)], axis=1).astype(
            jnp.bfloat16
        )

    def out_step(index):
        member, start, lane, column, sign = where_is(index)
        both = product(vt_ref[...], low_ref[keys, column])
        both += product(rvt_ref[member], low_ref[tail, column])
        out = jnp.where(mask_t_ref[:, lane] > 0.5, both[:hd], both[hd:])
        out = (out * inverse_ref[pl.ds(index, 1), :]).astype(jnp.bfloat16).astype(jnp.float32)
        wt = wt_ref[:, lane]
        reward_ref[pl.ds(member, 1), :] += jnp.sum(out * wt, axis=0, keepdims=True)
        delta_ref[pl.ds(index, 1), :] = jnp.sum(
            out * wt.astype(jnp.bfloat16).astype(jnp.float32), axis=0, keepdims=True
        )

    def back_step(index):
        member, start, lane, column, sign = where_is(index)
        delta = delta_ref[pl.ds(index, 1), :]
        ds = jnp.concatenate(
            [
                low_ref[strip, column] * (dp_ref[strip, lane] - delta).astype(jnp.bfloat16)
                for strip in strips
            ],
            axis=0,
        )
        dsr = low_ref[tail, column] * (drp_ref[member, :, lane] - delta).astype(jnp.bfloat16)
        ds_ref[keys, column] = ds
        ds_ref[tail, column] = dsr
        both = product(kt_ref[...], ds) + product(rkt_ref[member], dsr)
        gq = jnp.where(mask_t_ref[:, lane] > 0.5, both[:hd], both[hd:])
        gq = gq * (inverse_ref[pl.ds(index, 1), :] * (sign * scale))
        gqf_ref[member, pl.ds(start, TILE), :] = gq.T

    def resp_sums(part):
        left_ref, right_ref = ((ds_ref, q2i_ref), (low_ref, w2i_ref))[part]
        factor = 1.0 if part else scale
        for member in range(members):
            column = slice(member * rows, (member + 1) * rows)
            grf_ref[member, part] = product(left_ref[tail, column], right_ref[column, :]) * factor

    def sums(part):
        left_ref, right_ref = ((ds_ref, q2i_ref), (low_ref, w2i_ref))[part]
        factor = 1.0 if part else scale
        for kind, dz in ((3, 2), (1, 1), (2, -1), (0, 0)):
            row = pl.ds(pl.multiple_of(me.block(dz, 0) * block_rows, block_rows), 2 * block_rows)
            value = product(left_ref[row, :], right_ref[...]) * factor
            piece_ref[part, row, :] = value.astype(jnp.bfloat16)
            yield kind, dz

    def give(part, ready):
        index = 0
        for kind, dz in ready:
            for c in range(2) if kind else (1 - core,):
                push(
                    piece_ref.at[part, place(me.block(dz, c))],
                    got_ref.at[part, 2 * kind + core],
                    cb_send.at[part, index],
                    cb_recv.at[part, 2 * kind + core],
                    me.at(dz if kind != 3 else 4 * c - 2, 0, c),
                )
                index += 1
        got_ref[part, core] = piece_ref[part, place(me.block(0, core)), :]

    receive(0)
    for strip in strips:
        kt_ref[:, strip] = whole_ref[0, strip, :].astype(jnp.float32).T.astype(jnp.bfloat16)
    q_copy.wait()
    run(score_step, 0, count)
    value_pieces = list(sums(1))
    receive(1)
    give(1, value_pieces)
    for strip in strips:
        vt_ref[:, strip] = whole_ref[1, strip, :].astype(jnp.float32).T.astype(jnp.bfloat16)
    run(out_step, 0, count)

    ballot = vote_ref.at[me.tensor]
    for member in range(members):
        total = jnp.sum(reward_ref[member : member + 1, :], axis=1, keepdims=True)
        ballot[8 * member : 8 * (member + 1), :] = jnp.broadcast_to(total, (8, hd))
    for step, target in enumerate(peers):
        push(ballot, ballot, y_send.at[step], y_recv.at[step], target)
    dp_ref[...] = product(whole_ref[1], w2t_ref[...])
    run(back_step, 0, 6)

    for step in range(1, n_tensor):
        source = lax.rem(me.tensor + n_tensor - step, n_tensor)
        landed(vote_ref.at[source], y_recv.at[step - 1])
    reward = vote_ref[0]
    for index in range(1, n_tensor):
        reward = reward + vote_ref[index]
    reward = reward / positions
    margin = reward[8:16] - reward[:8]
    tiny = jnp.exp(-jnp.abs(margin))
    loss = jnp.maximum(margin, 0.0) + jnp.log1p(tiny)
    loss_ref[0] = loss[0, 0]
    sigmoid_gap = jnp.where(margin >= 0.0, 1.0, tiny) / (1.0 + tiny)
    gain = sigmoid_gap * (loss_scale / positions)
    gain_ref[core] = gain
    index = 0
    for kind, dz in ((3, 2), (1, 1), (2, -1), (0, 0)):
        for c in range(2) if kind else (1 - core,):
            push(
                gain_ref.at[core],
                gain_ref.at[2 * kind + core],
                g_send.at[index],
                g_recv.at[2 * kind + core],
                me.at(dz if kind != 3 else 4 * c - 2, 0, c),
            )
            index += 1

    names = [
        name(me.at(dz, 0, c)) for kind, dz in ((0, 0), (1, -1), (2, 1), (3, far)) for c in range(2)
    ]
    chunk = 16
    lanes = 128
    turns = (2, 1, 3, 0)
    sources = len(names)

    def factors():
        for kind in range(4):
            for c in range(2) if kind else (1 - core,):
                landed(gain_ref.at[2 * kind + c], g_recv.at[2 * kind + c])
        for a in range(LONG):
            for b in range(WIDE):
                prompt = slot(a, b)
                for source in range(sources):
                    row = (a * WIDE + b) * sources + source
                    share = jnp.where(names[source] == prompt, 1.0, 0.0)
                    factor_ref[row : row + 1, :] = gain_ref[source, :1, :] * share

    def add(left_ref, right_ref):
        return left_ref[...].astype(jnp.float32) + right_ref[...].astype(jnp.float32)

    def collect(part):
        for kind in range(4):
            for c in range(2) if kind else (1 - core,):
                landed(got_ref.at[part, 2 * kind + c], cb_recv.at[part, 2 * kind + c])

        for order, dzh in enumerate(turns):

            def select(index, carry):
                row = pl.ds(pl.multiple_of(index * chunk, chunk), chunk)
                for start in range(0, wide, lanes):
                    column = slice(start, start + lanes)
                    terms = [
                        got_ref[part, source, row, column].astype(jnp.float32)
                        for source in range(sources)
                    ]
                    for b in range(WIDE):
                        base = (dzh * WIDE + b) * sources
                        total = terms[0] * factor_ref[base : base + 1, :]
                        for source in range(1, sources):
                            at = base + source
                            total += terms[source] * factor_ref[at : at + 1, :]
                        dense_ref[part, dzh, b, row, column] = total.astype(jnp.bfloat16)
                return carry

            lax.fori_loop(0, block_rows // chunk, select, 0)
            for side, (dx, target) in enumerate(zip((1, 3, 2), sides)):
                push(
                    dense_ref.at[part, dzh, dx],
                    x2_ref.at[part, side, dzh],
                    xb_send.at[part, 4 * order + side],
                    xb_recv.at[part, 4 * order + side],
                    target,
                )

    def x_end(part, order):
        dzh = turns[order]
        for side in range(WIDE - 1):
            landed(x2_ref.at[part, side, dzh], xb_recv.at[part, 4 * order + side])
        total = add(x2_ref.at[part, 0, dzh], x2_ref.at[part, 1, dzh])
        total += add(x2_ref.at[part, 2, dzh], dense_ref.at[part, dzh, 0])
        sum_ref[part, dzh] = total.astype(jnp.bfloat16)

    def z_begin(part):
        for side, target in enumerate((up, down)):
            push(
                sum_ref.at[part, 2, parts[side]],
                z1_ref.at[part, side],
                zb_send.at[part, side],
                zb_recv.at[part, side],
                target,
            )

    def z_turn(part):
        for side, (dzh, target) in enumerate(((1, up), (3, down))):
            arrival = z1_ref.at[part, side]
            landed(arrival, zb_recv.at[part, side])
            block = sum_ref.at[part, dzh]
            section = block.at[parts[side]]
            section[...] = add(section, arrival).astype(jnp.bfloat16)
            push(
                block,
                z2_ref.at[part, side],
                zb_send.at[part, 2 + side],
                zb_recv.at[part, 2 + side],
                target,
            )

    def z_end(part):
        for side in range(2):
            landed(z2_ref.at[part, side], zb_recv.at[part, 2 + side])
        total = add(z2_ref.at[part, 0], z2_ref.at[part, 1])
        total += sum_ref[part, 0].astype(jnp.float32)
        sum_ref[part, 0] = total.astype(jnp.bfloat16)

    run(back_step, 6, 12)
    give(0, sums(0))
    factors()
    collect(1)
    resp_sums(0)
    resp_sums(1)

    def write_step(index):
        member, start, lane, column, sign = where_is(index)
        part = pl.ds(start, TILE)
        gq_ref[member, part, :] = (gqf_ref[member, part, :] * gain_ref[core, :1, :]).astype(
            jnp.bfloat16
        )

    run(write_step, 0, count)
    gq_copy = pltpu.make_async_copy(gq_ref, gq_hbm_ref, io_sem.at[1])
    gq_copy.start()
    gain2 = jnp.concatenate([gain[:1], gain[:1]], axis=1)
    for member in range(members):
        pair = [(grf_ref[member, part] * gain2).astype(jnp.bfloat16) for part in range(2)]
        for g in range(2):
            low = slice(g * hd, (g + 1) * hd)
            gr_ref[member, :, g, :, :] = jnp.stack([each[:, low] for each in pair], axis=1)
    x_end(1, 0)
    z_begin(1)
    collect(0)
    x_end(1, 1)
    x_end(1, 2)
    z_turn(1)
    x_end(1, 3)
    x_end(0, 0)
    z_begin(0)
    x_end(0, 1)
    x_end(0, 2)
    z_turn(0)
    x_end(0, 3)
    z_end(1)
    z_end(0)
    for g in range(2):
        low = slice(g * hd, (g + 1) * hd)
        owned_ref[:, g, :, :] = jnp.stack([sum_ref[part, 0, :, low] for part in range(2)], axis=1)
    gq_copy.wait()
    for copy in sent:
        copy.wait_send()


def pair_call(prompt_of, prompt_len, q, own, rkv, w, n_tensor):
    members, rows, hd = q.shape
    block_rows = own.shape[0]
    wide = 2 * hd
    positions = rkv.shape[1]
    heads = w.shape[0]
    n_prompt, n_resp = 2 * LONG, LONG * WIDE
    span = n_prompt * block_rows
    period = heads * TILE // math.gcd(heads, TILE)
    count = members * rows // TILE
    half = block_rows // 2
    vmem = pl.BlockSpec(memory_space=pltpu.VMEM)
    smem = pl.BlockSpec(memory_space=pltpu.SMEM)
    hbm = pl.BlockSpec(memory_space=pl.ANY)
    dma = pltpu.SemaphoreType.DMA
    low, full = jnp.bfloat16, jnp.float32

    def ways():
        return [dma((2, 4)), dma((2, 4)), dma((2, 16)), dma((2, 16)), dma((2, 8)), dma((2, 8))]

    return pl.pallas_call(
        pair_kernel,
        out_shape=(
            jax.ShapeDtypeStruct((members, rows, hd), low),
            jax.ShapeDtypeStruct((members, positions, 2, 2, hd), low),
            jax.ShapeDtypeStruct((block_rows, 2, 2, hd), low),
            jax.ShapeDtypeStruct((1,), full),
        ),
        in_specs=[smem, smem, hbm, vmem, vmem, vmem],
        out_specs=(hbm, vmem, vmem, smem),
        scratch_shapes=[
            pltpu.VMEM((n_resp, block_rows, wide), low),
            pltpu.VMEM((n_resp, block_rows, wide), low),
            pltpu.VMEM((2, n_prompt - 1, block_rows, wide), low),
            pltpu.VMEM((2, span, wide), low),
            pltpu.VMEM((members, rows, hd), low),
            pltpu.VMEM((members, rows, hd), low),
            pltpu.VMEM((period, hd), full),
            pltpu.VMEM((hd, period), full),
            pltpu.VMEM((period, hd), low),
            pltpu.VMEM((hd, period), full),
            pltpu.VMEM((period, wide), low),
            pltpu.VMEM((wide, period), low),
            pltpu.VMEM((members, positions, wide), low),
            pltpu.VMEM((members, positions, wide), low),
            pltpu.VMEM((wide, span), low),
            pltpu.VMEM((wide, span), low),
            pltpu.VMEM((members, wide, positions), low),
            pltpu.VMEM((members, wide, positions), low),
            pltpu.VMEM((span, period), full),
            pltpu.VMEM((members, positions, period), full),
            pltpu.VMEM((span + positions, count * TILE), low),
            pltpu.VMEM((span + positions, count * TILE), low),
            pltpu.VMEM((count * TILE, wide), low),
            pltpu.VMEM((count * TILE, wide), low),
            pltpu.VMEM((16, TILE), full),
            pltpu.VMEM((16, TILE), full),
            pltpu.VMEM((8, TILE), full),
            pltpu.VMEM((members, rows, hd), full),
            pltpu.VMEM((n_tensor, 8 * members, hd), full),
            pltpu.VMEM((n_prompt, 8, hd), full),
            pltpu.VMEM((n_prompt * n_resp, hd), full),
            pltpu.VMEM((2, span, wide), low),
            pltpu.VMEM((2, n_prompt, block_rows, wide), low),
            pltpu.VMEM((2, LONG, WIDE, block_rows, wide), low),
            pltpu.VMEM((2, LONG, block_rows, wide), low),
            pltpu.VMEM((members, 2, positions, wide), full),
            pltpu.VMEM((2, WIDE - 1, LONG, block_rows, wide), low),
            pltpu.VMEM((2, 2, half, wide), low),
            pltpu.VMEM((2, 2, block_rows, wide), low),
            *ways(),
            dma((n_tensor - 1,)),
            dma((n_tensor - 1,)),
            dma((n_prompt,)),
            dma((n_prompt,)),
            *ways(),
            dma((2,)),
        ],
        compiler_params=pltpu.CompilerParams(
            collective_id=0, has_side_effects=True, vmem_limit_bytes=56 * 2**20
        ),
    )(prompt_of, prompt_len, q, own, rkv, w)


def shards(queries, resp_kv, prompt_kv, prompt_of, prompt_len, reward_head):
    _, members, positions, heads, hd = queries.shape
    gq, gr, owned, pair_loss = pair_call(
        prompt_of,
        prompt_len,
        queries.reshape(members, positions * heads, hd),
        prompt_kv[0],
        resp_kv[0],
        reward_head,
        lax.axis_size("tensor"),
    )
    return (
        pair_loss,
        gq.reshape(queries.shape),
        gr.reshape(resp_kv.shape),
        owned.reshape(prompt_kv.shape),
    )


def solution(mesh):
    in_specs = (
        P(("prompt", "resp"), None, None, "tensor", None),
        P(("prompt", "resp"), None, None, "tensor", None, None),
        P("resp", "prompt", "tensor", None, None),
        P(),
        P(),
        P("tensor", None),
    )
    out_specs = (
        P(("prompt", "resp")),
        P(("prompt", "resp"), None, None, "tensor", None),
        P(("prompt", "resp"), None, None, "tensor", None, None),
        P("resp", "prompt", "tensor", None, None),
    )
    return jax.shard_map(shards, mesh=mesh, in_specs=in_specs, out_specs=out_specs, check_vma=False)
```
